256 devices in a mesh: row: 32 (over z, x), col: 2 (over core), depth: 4 (over y).
Axes of the slice: x: 4, y: 4, z: 8, core: 2. Of those that a mesh axis runs over, the one named last changes fastest.
Arguments:
- attn_out: bfloat16 [32768, 3072], P(('depth', 'row'), 'col'), may hold values from -24 to 24
- w_out: bfloat16 [3072, 3072], P('row', 'col'), may hold values from -0.21875 to 0.21875
- cotangent: bfloat16 [32768, 3072], P(('depth', 'row'), 'col'), may hold values from -6 to 6
Outputs:
- projected: bfloat16 [32768, 3072], P(('depth', 'row'), 'col')
- input_grad: bfloat16 [32768, 3072], P(('depth', 'row'), 'col')
- weight_grad: float32 [3072, 3072], P('row', 'col')
The draws below stay inside these ranges and needn't reach their ends.
All inputs are finite; a program needn't handle non-finite values.
Results may differ from the reference program's by a relative error of at most 0.001.
Values may be sent and summed in bfloat16 or wider, within the bound.
A program may use at most 128 MiB of HBM per device.

```python
import math
import jax
import jax.numpy as jnp

HD = 3072
DM = 3072
TOKENS = 32768


def with_spikes(drawn, own_key, source, target, parts, factor):
    def block_of(dim):
        return (jnp.arange(drawn.shape[dim]) // (drawn.shape[dim] // parts)).reshape((-1,) + (1,) * (drawn.ndim - 1 - dim))

    first = jax.random.permutation(own_key, parts)[block_of(target)]
    other_side = (block_of(target) + parts // 2) % parts
    return jnp.where((block_of(source) == first) | (block_of(source) == other_side), factor * drawn, drawn)


def levels(rng, shape, pieces, least, top_value):
    factor_of = 1.0
    for axis_at, shards_of in pieces:
        steps = jax.random.uniform(jax.random.fold_in(jax.random.fold_in(rng, 6), axis_at), (shards_of,), jnp.float32, least / len(pieces), top_value / len(pieces))
        factor_of = factor_of * jnp.repeat(jnp.exp(steps), shape[axis_at] // shards_of).reshape((-1,) + (1,) * (len(shape) - 1 - axis_at))
    return factor_of


def centred(rng, shape, spread, reach, split=(), held_as=jnp.bfloat16):
    drawn = jax.random.normal(rng, shape, jnp.float32) * spread
    if len(split) > 0:
        drawn = levels(rng, shape, split, -0.22, 0.18) * drawn
    return jnp.clip(drawn, min=-reach, max=reach).astype(held_as)


def heavy_noise(key, dims, scale, reach, shards, heavy, held_as=jnp.bfloat16):
    entries = scale * jax.random.normal(key, dims, jnp.float32)
    if shards:
        entries = entries * levels(key, dims, shards, -0.22, 0.18)
    return jnp.clip(with_spikes(entries, jax.random.fold_in(key, 3), *heavy), -reach, reach).astype(held_as)


def setup_inputs(seed: int = 0) -> dict:
    keys = jax.random.split(jax.random.key(seed), 4)
    attn_out = heavy_noise(keys[0], (TOKENS, HD), 1.0, 24.0, ((0, 128), (1, 2)), (0, 1, 128, 5.5))
    w_out = heavy_noise(keys[1], (HD, DM), HD ** -0.5, 0.21875, ((0, 32), (1, 2)), (1, 0, 32, 2.75))
    cotangent = centred(keys[2], (TOKENS, DM), 1.0, 6.0, ((0, 128), (1, 2)))
    return dict(attn_out=attn_out, w_out=w_out, cotangent=cotangent)


def reference(attn_out, w_out, cotangent):
    projected = jnp.dot(attn_out, w_out, preferred_element_type=jnp.float32).astype(jnp.bfloat16)
    input_grad = jnp.dot(cotangent, w_out.T, preferred_element_type=jnp.float32).astype(jnp.bfloat16)
    total = jnp.dot(attn_out.T, cotangent, preferred_element_type=jnp.float32)
    weight_grad = total * (1.0 / math.sqrt(TOKENS))
    return (projected, input_grad, weight_grad)
```

```python
import math

import jax
import jax.numpy as jnp
from jax import lax
from jax.experimental import pallas as pl
from jax.experimental.pallas import tpu as pltpu
from jax.sharding import PartitionSpec as P

MESH = pl.DeviceIdType.MESH
NZ, NX, NY = 8, 4, 4
TOK, HALF, BLK = 256, 1536, 96
MAIN, TILE = 1024, 128
WIDE = MAIN + TILE
QUART = HALF // NY
R1 = 64
S1 = 48
F32, BF16 = jnp.float32, jnp.bfloat16
N_MSG = 200


def kernel(attn, w, cot, proj, igrad, wgrad, A, CQ, Wp, Wr, cotp, G, bo, bm, br,
           xa, xb, za, zb, za4, ya, yb, yxa, yxb, send, recv):
    row, c, y = lax.axis_index("row"), lax.axis_index("col"), lax.axis_index("depth")
    z, x = row // NX, lax.rem(row, NX)

    def zz(k):
        return lax.rem(z + (k % NZ), NZ)

    def xx(k):
        return lax.rem(x + (k % NX), NX)

    def yy(k):
        return lax.rem(y + (k % NY), NY)

    zp, zm = (zz(1) * NX + x, c, y), (zz(-1) * NX + x, c, y)
    xp, xm = (z * NX + xx(1), c, y), (z * NX + xx(-1), c, y)
    yp, ym, y2 = (row, c, yy(1)), (row, c, yy(-1)), (row, c, yy(2))
    core = (row, 1 - c, y)
    started = []

    def push(src, dst, dev):
        k = len(started)
        copy = pltpu.make_async_remote_copy(
            src_ref=src, dst_ref=dst, send_sem=send.at[k], recv_sem=recv.at[k], device_id=dev, device_id_type=MESH
        )
        copy.start()
        started.append(copy)
        return copy

    Wp[z, x, :, 0:MAIN] = w[:, 0:MAIN]
    Wp[z, x, :, MAIN:WIDE] = w[:, pl.ds(pl.multiple_of(MAIN + TILE * y, TILE), TILE)]

    barrier = pltpu.get_barrier_semaphore()
    for dev in (zp, zm, xp, xm, yp, ym, y2, core):
        pl.semaphore_signal(barrier, inc=1, device_id=dev, device_id_type=MESH)
    pl.semaphore_wait(barrier, 8)

    def ablk(k, h, r0, n):
        return A.at[pl.ds(pl.multiple_of(yy(k) * TOK + r0, 128), n), pl.ds(pl.multiple_of(h * HALF, 128), HALF)]

    HT = TOK // 2
    wz, wx, wr, wy = {}, {}, {}, {}

    def blk(k, r0, n):
        return Wp.at[zz(k), x, pl.ds(r0, n), :]

    def pushz(step):
        k = step - 1
        if step < 4:
            wz[step, 0] = push(blk(-k, 0, R1), blk(-k, 0, R1), zp)
            wz[step, 1] = push(blk(k, 0, R1), blk(k, 0, R1), zm)
        else:
            wz[step, 0] = push(blk(-k, 0, R1 // 2), blk(-k, 0, R1 // 2), zp)
            wz[step, 1] = push(blk(k, R1 // 2, R1 // 2), blk(k, R1 // 2, R1 // 2), zm)

    def waitz(step):
        wz[step, 0].wait_recv()
        wz[step, 1].wait_recv()

    def pushx(k):
        wx[k, 0] = push(blk(k, 0, R1), blk(k, 0, R1), xp)
        wx[k, 1] = push(blk(k, 0, R1), blk(k, 0, R1), xm)

    def relayx(k):
        h = R1 // 2
        wx[k, 0].wait_recv()
        left = Wp.at[zz(k), xx(-1), pl.ds(0, h), :]
        wx[k, 2] = push(left, left, xp)
        wx[k, 1].wait_recv()
        right = Wp.at[zz(k), xx(1), pl.ds(h, h), :]
        wx[k, 3] = push(right, right, xm)

    def waitx(k):
        wx[k, 2].wait_recv()
        wx[k, 3].wait_recv()

    R2 = BLK - R1

    def rblk(k, r0, n):
        return Wp.at[zz(k), :, pl.ds(r0, n), :]

    def pushr(step):
        k = step - 1
        if step < 4:
            wr[step, 0] = push(rblk(-k, R1, R2), rblk(-k, R1, R2), zp)
            wr[step, 1] = push(rblk(k, R1, R2), rblk(k, R1, R2), zm)
        else:
            h = R2 // 2
            wr[step, 0] = push(rblk(-k, R1, h), rblk(-k, R1, h), zp)
            wr[step, 1] = push(rblk(k, R1 + h, h), rblk(k, R1 + h, h), zm)

    def waitr(step):
        wr[step, 0].wait_recv()
        wr[step, 1].wait_recv()

    def wtile(k, j):
        return Wr.at[zz(k), :, :, pl.ds(j * TILE, TILE)]

    def pushy(k):
        src = Wp.at[zz(k), :, :, pl.ds(MAIN, TILE)]
        wy[k, 0] = push(src, wtile(k, 0), yp)
        wy[k, 1] = push(src, wtile(k, 1), ym)

    def relayy(k):
        if k % 2 == 0:
            wy[k, 0].wait_recv()
            wy[k, 2] = push(wtile(k, 0), wtile(k, 2), yp)
        else:
            wy[k, 1].wait_recv()
            wy[k, 2] = push(wtile(k, 1), wtile(k, 2), ym)

    def waity(k):
        wy[k, 1 - k % 2].wait_recv()
        wy[k, 2].wait_recv()

    pushz(1)
    X1 = Wp.at[z, x, pl.ds(R1, R2), :]
    wxr = [push(X1, X1, xp), push(X1, X1, xm)]
    at = {}
    at["ap"] = push(attn.at[pl.ds(0, HT)], ablk(0, c, 0, HT), yp)
    at["bm"] = push(attn.at[pl.ds(HT, HT)], ablk(0, c, HT, HT), ym)
    pushx(0)
    at["bp"] = push(attn.at[pl.ds(HT, HT)], ablk(0, c, HT, HT), yp)
    at["am"] = push(attn.at[pl.ds(0, HT)], ablk(0, c, 0, HT), ym)
    ct = []
    for k, dev in ((1, yp), (-1, ym), (2, y2)):
        q = cot.at[:, pl.ds(pl.multiple_of(yy(k) * QUART, 128), QUART)]
        ct.append(push(q, CQ.at[pl.ds(pl.multiple_of(y * TOK, TOK), TOK), :], dev))
    cc = [push(attn, ablk(0, c, 0, TOK), core)]
    A[pl.ds(pl.multiple_of(y * TOK, TOK), TOK), pl.ds(pl.multiple_of(c * HALF, 128), HALF)] = attn[...]
    CQ[pl.ds(pl.multiple_of(y * TOK, TOK), TOK), :] = cot[:, pl.ds(pl.multiple_of(y * QUART, 128), QUART)]
    cotp[:, 0:MAIN] = cot[:, 0:MAIN]
    for j, k in enumerate((0, -1, 1, 2)):
        cotp[:, MAIN + j * TILE:MAIN + (j + 1) * TILE] = cot[:, pl.ds(pl.multiple_of(MAIN + yy(k) * TILE, TILE), TILE)]

    waitz(1)
    pushz(2)
    pushx(-1)
    pushx(1)
    wxr[0].wait_recv()
    h = R2 // 2
    left = Wp.at[z, xx(-1), pl.ds(R1, h), :]
    wxr.append(push(left, left, xp))
    wxr[1].wait_recv()
    right = Wp.at[z, xx(1), pl.ds(R1 + h, h), :]
    wxr.append(push(right, right, xm))
    relayx(0)
    waitz(2)
    pushz(3)
    pushx(-2)
    pushx(2)
    at["ap"].wait_recv()
    at["rp"] = push(ablk(-1, c, 0, HT), ablk(-1, c, 0, HT), yp)
    at["bm"].wait_recv()
    at["rm"] = push(ablk(1, c, HT, HT), ablk(1, c, HT, HT), ym)
    wxr[2].wait_recv()
    wxr[3].wait_recv()
    pushr(1)
    waitz(3)
    pushz(4)
    pushx(-3)
    pushx(3)
    relayx(-1)
    relayx(1)
    waitr(1)
    pushr(2)
    at["bp"].wait_recv()
    cc.append(push(ablk(-1, c, 0, TOK), ablk(-1, c, 0, TOK), core))
    at["am"].wait_recv()
    cc.append(push(ablk(1, c, 0, TOK), ablk(1, c, 0, TOK), core))
    waitz(4)
    pushx(4)
    waitx(0)
    pushy(0)
    relayx(-2)
    relayx(2)
    waitr(2)
    pushr(3)
    relayx(-3)
    relayx(3)
    waitr(3)
    pushr(4)
    for copy in ct:
        copy.wait_recv()
    at["rp"].wait_recv()
    at["rm"].wait_recv()
    cc.append(push(ablk(2, c, 0, TOK), ablk(2, c, 0, TOK), core))
    waitx(-1)
    pushy(-1)
    waitx(1)
    pushy(1)
    relayx(4)
    for copy in cc:
        copy.wait_recv()

    def term(k):
        zi = zz(k)
        a = A[:, pl.ds(pl.multiple_of(zi * NX * BLK, 128), NX * BLK)]
        g = lax.dot_general(a, CQ[...], (((0,), (0,)), ((), ())), preferred_element_type=F32)
        G[zi] = g.reshape(NX, BLK, QUART)

    H1 = S1 // 2
    S2 = BLK - S1
    H2 = S2 // 2
    M2 = S1 + H2
    gx, gz, gy, gyx = {}, {}, {}, {}

    def sumx1(k):
        gx[k, 0] = push(G.at[zz(k), xx(2), pl.ds(0, H1)], xa.at[k % NZ, 0], xp)
        gx[k, 1] = push(G.at[zz(k), xx(2), pl.ds(H1, H1)], xa.at[k % NZ, 1], xm)

    def sumx2(k):
        gx[k, 0].wait_recv()
        G[zz(k), xx(1), 0:H1] += xa[k % NZ, 0]
        gx[k, 2] = push(G.at[zz(k), xx(1), pl.ds(0, S1)], xb.at[k % NZ, 0], xp)
        gx[k, 1].wait_recv()
        G[zz(k), xx(-1), H1:S1] += xa[k % NZ, 1]
        gx[k, 3] = push(G.at[zz(k), xx(-1), pl.ds(0, S1)], xb.at[k % NZ, 1], xm)

    def sumx3(k):
        gx[k, 2].wait_recv()
        gx[k, 3].wait_recv()
        G[zz(k), x, 0:S1] += xb[k % NZ, 0] + xb[k % NZ, 1]

    def sumz(step):
        if step == 1:
            gz[1, 0] = push(G.at[zz(4), x, pl.ds(0, H1)], za4.at[0], zp)
            gz[1, 1] = push(G.at[zz(4), x, pl.ds(H1, H1)], za4.at[1], zm)
            return
        gz[step - 1, 0].wait_recv()
        gz[step - 1, 1].wait_recv()
        if step == 2:
            G[zz(3), x, 0:H1] += za4[0]
            G[zz(-3), x, H1:S1] += za4[1]
        elif step < 5:
            G[zz(5 - step), x, 0:S1] += za[step - 3, 0]
            G[zz(step - 5), x, 0:S1] += za[step - 3, 1]
        else:
            G[z, x, 0:S1] += za[2, 0] + za[2, 1]
            return
        gz[step, 0] = push(G.at[zz(5 - step), x, pl.ds(0, S1)], za.at[step - 2, 0], zp)
        gz[step, 1] = push(G.at[zz(step - 5), x, pl.ds(0, S1)], za.at[step - 2, 1], zm)

    def sumy(step):
        if step == 1:
            gy[1, 0] = push(G.at[zz(4), :, pl.ds(S1, H2)], yb.at[0], zp)
            gy[1, 1] = push(G.at[zz(4), :, pl.ds(M2, H2)], yb.at[1], zm)
            return
        gy[step - 1, 0].wait_recv()
        gy[step - 1, 1].wait_recv()
        if step == 2:
            G[zz(3), :, S1:M2] += yb[0]
            G[zz(-3), :, M2:BLK] += yb[1]
        elif step < 5:
            G[zz(5 - step), :, S1:BLK] += ya[step - 3, 0]
            G[zz(step - 5), :, S1:BLK] += ya[step - 3, 1]
        else:
            G[z, :, S1:BLK] += ya[2, 0] + ya[2, 1]
            return
        gy[step, 0] = push(G.at[zz(5 - step), :, pl.ds(S1, S2)], ya.at[step - 2, 0], zp)
        gy[step, 1] = push(G.at[zz(step - 5), :, pl.ds(S1, S2)], ya.at[step - 2, 1], zm)

    def fwd(lo, width, src, at_col):
        a = A[pl.ds(pl.multiple_of(y * TOK, TOK), TOK), :]
        p = jnp.dot(a, src[:, :, :, lo:lo + width].reshape(NZ * NX * BLK, width), preferred_element_type=F32)
        proj[:, pl.ds(at_col, width)] = p.astype(BF16)

    def col(k):
        return pl.multiple_of(MAIN + yy(k) * TILE, TILE)

    def bwd(zi):
        return lax.dot_general(
            cotp[:, 0:WIDE], Wp[zi].reshape(NX * BLK, WIDE), (((1,), (1,)), ((), ())), preferred_element_type=F32
        )

    def bwd_rest(zi):
        return lax.dot_general(
            cotp[:, WIDE:], Wr[zi].reshape(NX * BLK, HALF - WIDE), (((1,), (1,)), ((), ())), preferred_element_type=F32
        )

    term(4)
    sumy(1)
    sumx1(4)
    term(3)
    sumx1(3)
    term(-3)
    sumx1(-3)
    term(2)
    term(-2)
    waitr(4)
    waitx(-2)
    pushy(-2)
    waitx(2)
    pushy(2)
    waitx(-3)
    pushy(-3)
    waitx(3)
    pushy(3)
    waitx(4)
    pushy(4)
    sumx2(4)
    sumy(2)
    sumx1(2)
    sumx1(-2)
    term(1)
    term(-1)
    sumx2(3)
    sumx2(-3)
    sumx1(1)
    sumx1(-1)
    relayy(0)
    relayy(-1)
    relayy(1)
    term(0)
    sumx3(4)
    sumz(1)
    fwd(0, 256, Wp, 0)
    sumx1(0)
    sumy(3)
    sumx2(2)
    sumx2(-2)
    sumx3(3)
    sumx3(-3)
    sumz(2)
    relayy(-2)
    relayy(2)
    fwd(256, 256, Wp, 256)
    fwd(512, 256, Wp, 512)
    sumx2(1)
    sumx2(-1)
    sumy(4)
    sumx3(2)
    sumx3(-2)
    sumz(3)
    relayy(-3)
    relayy(3)
    fwd(768, 256, Wp, 768)
    fwd(MAIN, TILE, Wp, col(0))
    sumx2(0)
    sumx3(1)
    sumx3(-1)
    sumz(4)
    relayy(4)
    for j in range(4):
        bo[j] = bwd(4 * (1 - c) + j)
    sumy(5)
    gyx[0] = push(G.at[z, xx(2), pl.ds(S1, H2)], yxa.at[0], xp)
    gyx[1] = push(G.at[z, xx(2), pl.ds(M2, H2)], yxa.at[1], xm)
    for j in range(4):
        bm[j] = bwd(4 * c + j)
    gyx[0].wait_recv()
    G[z, xx(1), S1:M2] += yxa[0]
    gyx[2] = push(G.at[z, xx(1), pl.ds(S1, S2)], yxb.at[0], xp)
    gyx[1].wait_recv()
    G[z, xx(-1), M2:BLK] += yxa[1]
    gyx[3] = push(G.at[z, xx(-1), pl.ds(S1, S2)], yxb.at[1], xm)
    sumx3(0)
    sumz(5)
    scale = 1.0 / math.sqrt(TOK * NZ * NX * NY)
    mine = pl.ds(pl.multiple_of(y * QUART, 128), QUART)
    wgrad[0:S1, mine] = G[z, x, 0:S1] * scale
    last = [push(wgrad.at[pl.ds(0, S1), mine], wgrad.at[pl.ds(0, S1), mine], dev) for dev in (yp, ym, y2)]
    gyx[2].wait_recv()
    gyx[3].wait_recv()
    wgrad[S1:BLK, mine] = (G[z, x, S1:BLK] + (yxb[0] + yxb[1])) * scale
    last += [push(wgrad.at[pl.ds(S1, S2), mine], wgrad.at[pl.ds(S1, S2), mine], dev) for dev in (yp, ym, y2)]
    for k in (0, -1, 1, -2, 2, -3, 3, 4):
        waity(k)
    back = []
    for j in range(4):
        bo[j] += bwd_rest(4 * (1 - c) + j)
        back.append(push(bo.at[j], br.at[j], core))
    for j in range(4):
        bm[j] += bwd_rest(4 * c + j)
    for j, k in enumerate((-1, 1, 2)):
        fwd(j * TILE, TILE, Wr, col(k))
    for j in range(4):
        back[j].wait_recv()
        igrad[:, j * NX * BLK:(j + 1) * NX * BLK] = (bm[j] + br[j]).astype(BF16)
    for copy in last:
        copy.wait_recv()
    for copy in started:
        copy.wait_send()


def body(attn, w, cot):
    h1, s2, h2 = S1 // 2, BLK - S1, (BLK - S1) // 2
    vmem = pl.BlockSpec(memory_space=pltpu.VMEM)
    return pl.pallas_call(
        kernel,
        out_shape=(
            jax.ShapeDtypeStruct((TOK, HALF), BF16),
            jax.ShapeDtypeStruct((TOK, HALF), BF16),
            jax.ShapeDtypeStruct((BLK, HALF), F32),
        ),
        in_specs=[vmem] * 3,
        out_specs=(vmem,) * 3,
        scratch_shapes=[
            pltpu.VMEM((NY * TOK, 2 * HALF), BF16),
            pltpu.VMEM((NY * TOK, QUART), BF16),
            pltpu.VMEM((NZ, NX, BLK, WIDE), BF16),
            pltpu.VMEM((NZ, NX, BLK, HALF - WIDE), BF16),
            pltpu.VMEM((TOK, HALF), BF16),
            pltpu.VMEM((NZ, NX, BLK, QUART), F32),
            pltpu.VMEM((4, TOK, NX * BLK), F32),
            pltpu.VMEM((4, TOK, NX * BLK), F32),
            pltpu.VMEM((4, TOK, NX * BLK), F32),
            pltpu.VMEM((NZ, 2, h1, QUART), F32),
            pltpu.VMEM((NZ, 2, S1, QUART), F32),
            pltpu.VMEM((3, 2, S1, QUART), F32),
            pltpu.VMEM((2, h1, QUART), F32),
            pltpu.VMEM((2, h1, QUART), F32),
            pltpu.VMEM((3, 2, NX, s2, QUART), F32),
            pltpu.VMEM((2, NX, h2, QUART), F32),
            pltpu.VMEM((2, h2, QUART), F32),
            pltpu.VMEM((2, s2, QUART), F32),
            pltpu.SemaphoreType.DMA((N_MSG,)),
            pltpu.SemaphoreType.DMA((N_MSG,)),
        ],
        compiler_params=pltpu.CompilerParams(
            collective_id=0, has_side_effects=True, vmem_limit_bytes=56 * 2**20
        ),
        name="projection",
    )(attn, w, cot)


def solution(mesh):
    in_specs = (P(("depth", "row"), "col"), P("row", "col"), P(("depth", "row"), "col"))
    out_specs = (P(("depth", "row"), "col"), P(("depth", "row"), "col"), P("row", "col"))
    return jax.shard_map(body, mesh=mesh, in_specs=in_specs, out_specs=out_specs, check_vma=False)
```

```python
import math

import jax
import jax.numpy as jnp
from jax import lax
from jax.experimental import pallas as pl
from jax.experimental.pallas import tpu as pltpu
from jax.sharding import PartitionSpec as P

MESH = pl.DeviceIdType.MESH
NZ, NX, NY = 8, 4, 4
TOK, HALF, BLK = 256, 1536, 96
MAIN, TILE = 1024, 128
WIDE = MAIN + TILE
QUART = HALF // NY
R1 = 64
R2 = BLK - R1
S1 = 48
S2 = BLK - S1
H1, H2 = S1 // 2, S2 // 2
M2 = S1 + H2
HT = TOK // 2
ZBLK = NX * BLK
F32, BF16 = jnp.float32, jnp.bfloat16
N_MSG = 208


def kernel(attn, w, cot, proj, igrad, wgrad, A, CQ, Wp, Wr, cotp, G, bo, bm, br,
           xa, xb, za, za4, ya, yb, yxa, yxb, send, recv):
    row, c, y = lax.axis_index("row"), lax.axis_index("col"), lax.axis_index("depth")
    z, x = row // NX, lax.rem(row, NX)

    def zz(k):
        return lax.rem(z + (k % NZ), NZ)

    def xx(k):
        return lax.rem(x + (k % NX), NX)

    def yy(k):
        return lax.rem(y + (k % NY), NY)

    zp, zm = (zz(1) * NX + x, c, y), (zz(-1) * NX + x, c, y)
    xp, xm = (z * NX + xx(1), c, y), (z * NX + xx(-1), c, y)
    yp, ym, y2 = (row, c, yy(1)), (row, c, yy(-1)), (row, c, yy(2))
    core = (row, 1 - c, y)
    started = []

    def push(src, dst, dev):
        k = len(started)
        copy = pltpu.make_async_remote_copy(
            src_ref=src, dst_ref=dst, send_sem=send.at[k], recv_sem=recv.at[k], device_id=dev, device_id_type=MESH
        )
        copy.start()
        started.append(copy)
        return copy

    def same(ref, dev):
        return push(ref, ref, dev)

    at, ct, cc, wz, wx, wr, wxr, wy = {}, {}, {}, {}, {}, {}, {}, {}
    gx, gz, gy, gyx, last, back = {}, {}, {}, {}, {}, {}

    def ablk(k, h, r0, n):
        return A.at[pl.ds(pl.multiple_of(yy(k) * TOK + r0, 128), n), pl.ds(pl.multiple_of(h * HALF, 128), HALF)]

    def att(i):
        r0 = i * HT
        at[i, 0] = push(attn.at[pl.ds(r0, HT)], ablk(0, c, r0, HT), yp)
        r0 = (1 - i) * HT
        at[i, 1] = push(attn.at[pl.ds(r0, HT)], ablk(0, c, r0, HT), ym)

    def att_on(i):
        at[0, i].wait_recv()
        k = -1 if i == 0 else 1
        at[2, i] = same(ablk(k, c, i * HT, HT), yp if i == 0 else ym)

    def cots(k):
        q = cot.at[:, pl.ds(pl.multiple_of(yy(k) * QUART, 128), QUART)]
        ct[k] = push(q, CQ.at[pl.ds(pl.multiple_of(y * TOK, TOK), TOK), :], {1: yp, -1: ym, 2: y2}[k])

    def cots_in():
        for k in (1, -1, 2):
            ct[k].wait_recv()

    def own():
        cc[0] = push(attn, ablk(0, c, 0, TOK), core)
        A[pl.ds(pl.multiple_of(y * TOK, TOK), TOK), pl.ds(pl.multiple_of(c * HALF, 128), HALF)] = attn[...]
        CQ[pl.ds(pl.multiple_of(y * TOK, TOK), TOK), :] = cot[:, pl.ds(pl.multiple_of(y * QUART, 128), QUART)]
        cotp[:, 0:MAIN] = cot[:, 0:MAIN]
        for j, k in enumerate((0, -1, 1, 2)):
            lane = pl.multiple_of(MAIN + yy(k) * TILE, TILE)
            cotp[:, MAIN + j * TILE:MAIN + (j + 1) * TILE] = cot[:, pl.ds(lane, TILE)]

    def cross(k):
        if k == 2:
            at[2, 0].wait_recv()
            at[2, 1].wait_recv()
        else:
            at[1, 0 if k == -1 else 1].wait_recv()
        cc[k] = same(ablk(k, c, 0, TOK), core)

    def cross_in(k):
        cc[k].wait_recv()

    def blk(k, r0, n):
        return Wp.at[zz(k), x, pl.ds(r0, n), :]

    def zpush(step):
        k, h = step - 1, R1 // 2
        if step < 4:
            wz[step, 0] = same(blk(-k, 0, R1), zp)
            wz[step, 1] = same(blk(k, 0, R1), zm)
        else:
            wz[step, 0] = same(blk(-k, 0, h), zp)
            wz[step, 1] = same(blk(k, h, h), zm)

    def zstep(step):
        wz[step, 0].wait_recv()
        wz[step, 1].wait_recv()
        if step < 4:
            zpush(step + 1)

    def xpush(k):
        wx[k, 0] = same(blk(k, 0, R1), xp)
        wx[k, 1] = same(blk(k, 0, R1), xm)

    def xstep(k):
        h = R1 // 2
        wx[k, 0].wait_recv()
        wx[k, 2] = same(Wp.at[zz(k), xx(-1), pl.ds(0, h), :], xp)
        wx[k, 1].wait_recv()
        wx[k, 3] = same(Wp.at[zz(k), xx(1), pl.ds(h, h), :], xm)

    def xlast(k):
        wx[k, 2].wait_recv()
        wx[k, 3].wait_recv()

    def rx():
        mine = Wp.at[z, x, pl.ds(R1, R2), :]
        wxr[0] = same(mine, xp)
        wxr[1] = same(mine, xm)

    def rx_on():
        h = R2 // 2
        wxr[0].wait_recv()
        wxr[2] = same(Wp.at[z, xx(-1), pl.ds(R1, h), :], xp)
        wxr[1].wait_recv()
        wxr[3] = same(Wp.at[z, xx(1), pl.ds(R1 + h, h), :], xm)

    def rx_in():
        wxr[2].wait_recv()
        wxr[3].wait_recv()

    def rpush(step, j):
        k, h = step - 1, R2 // 2
        if step < 4:
            wr[step, j, 0] = same(Wp.at[zz(-k), xx(j), pl.ds(R1, R2), :], zp)
            wr[step, j, 1] = same(Wp.at[zz(k), xx(j), pl.ds(R1, R2), :], zm)
        else:
            wr[step, j, 0] = same(Wp.at[zz(-k), xx(j), pl.ds(R1, h), :], zp)
            wr[step, j, 1] = same(Wp.at[zz(k), xx(j), pl.ds(R1 + h, h), :], zm)

    def rstep(step, j):
        wr[step, j, 0].wait_recv()
        wr[step, j, 1].wait_recv()
        if step < 4:
            rpush(step + 1, j)

    def wtile(k, j):
        return Wr.at[zz(k), :, :, pl.ds(j * TILE, TILE)]

    def ypush(k):
        src = Wp.at[zz(k), :, :, pl.ds(MAIN, TILE)]
        wy[k, 0] = push(src, wtile(k, 0), yp)
        wy[k, 1] = push(src, wtile(k, 1), ym)

    def ystep(k):
        j = k % 2
        wy[k, j].wait_recv()
        wy[k, 2] = push(wtile(k, j), wtile(k, 2), ym if j else yp)

    def ylast(k):
        wy[k, 1 - k % 2].wait_recv()
        wy[k, 2].wait_recv()

    def term(k):
        zi = zz(k)
        a = A[:, pl.ds(pl.multiple_of(zi * ZBLK, 128), ZBLK)]
        g = lax.dot_general(a, CQ[...], (((0,), (0,)), ((), ())), preferred_element_type=F32)
        G[zi] = g.reshape(NX, BLK, QUART)

    def sumx(k):
        gx[k, 0] = push(G.at[zz(k), xx(2), pl.ds(0, H1)], xa.at[k % NZ, 0], xp)
        gx[k, 1] = push(G.at[zz(k), xx(2), pl.ds(H1, H1)], xa.at[k % NZ, 1], xm)

    def sumx_on(k):
        gx[k, 0].wait_recv()
        G[zz(k), xx(1), 0:H1] += xa[k % NZ, 0]
        gx[k, 2] = push(G.at[zz(k), xx(1), pl.ds(0, S1)], xb.at[k % NZ, 0], xp)
        gx[k, 1].wait_recv()
        G[zz(k), xx(-1), H1:S1] += xa[k % NZ, 1]
        gx[k, 3] = push(G.at[zz(k), xx(-1), pl.ds(0, S1)], xb.at[k % NZ, 1], xm)

    def sumx_in(k):
        gx[k, 2].wait_recv()
        gx[k, 3].wait_recv()
        G[zz(k), x, 0:S1] += xb[k % NZ, 0] + xb[k % NZ, 1]

    def sumz(step):
        if step == 1:
            gz[1, 0] = push(G.at[zz(4), x, pl.ds(0, H1)], za4.at[0], zp)
            gz[1, 1] = push(G.at[zz(4), x, pl.ds(H1, H1)], za4.at[1], zm)
            return
        gz[step - 1, 0].wait_recv()
        gz[step - 1, 1].wait_recv()
        if step == 2:
            G[zz(3), x, 0:H1] += za4[0]
            G[zz(-3), x, H1:S1] += za4[1]
        elif step < 5:
            G[zz(5 - step), x, 0:S1] += za[step - 3, 0]
            G[zz(step - 5), x, 0:S1] += za[step - 3, 1]
        else:
            G[z, x, 0:S1] += za[2, 0] + za[2, 1]
            return
        gz[step, 0] = push(G.at[zz(5 - step), x, pl.ds(0, S1)], za.at[step - 2, 0], zp)
        gz[step, 1] = push(G.at[zz(step - 5), x, pl.ds(0, S1)], za.at[step - 2, 1], zm)

    def sumy(step, j):
        i, d = xx(j), j % NX
        if step == 1:
            gy[1, j, 0] = push(G.at[zz(4), i, pl.ds(S1, H2)], yb.at[0, d], zp)
            gy[1, j, 1] = push(G.at[zz(4), i, pl.ds(M2, H2)], yb.at[1, d], zm)
            return
        gy[step - 1, j, 0].wait_recv()
        gy[step - 1, j, 1].wait_recv()
        if step == 2:
            G[zz(3), i, S1:M2] += yb[0, d]
            G[zz(-3), i, M2:BLK] += yb[1, d]
        elif step < 5:
            G[zz(5 - step), i, S1:BLK] += ya[step - 3, 0, d]
            G[zz(step - 5), i, S1:BLK] += ya[step - 3, 1, d]
        else:
            G[z, i, S1:BLK] += ya[2, 0, d] + ya[2, 1, d]
            return
        gy[step, j, 0] = push(G.at[zz(5 - step), i, pl.ds(S1, S2)], ya.at[step - 2, 0, d], zp)
        gy[step, j, 1] = push(G.at[zz(step - 5), i, pl.ds(S1, S2)], ya.at[step - 2, 1, d], zm)

    def sumyx():
        gyx[0] = push(G.at[z, xx(2), pl.ds(S1, H2)], yxa.at[0], xp)
        gyx[1] = push(G.at[z, xx(2), pl.ds(M2, H2)], yxa.at[1], xm)

    def sumyx_on():
        gyx[0].wait_recv()
        G[z, xx(1), S1:M2] += yxa[0]
        gyx[2] = push(G.at[z, xx(1), pl.ds(S1, S2)], yxb.at[0], xp)
        gyx[1].wait_recv()
        G[z, xx(-1), M2:BLK] += yxa[1]
        gyx[3] = push(G.at[z, xx(-1), pl.ds(S1, S2)], yxb.at[1], xm)

    def wout(r0, n, g):
        at_y = pl.ds(pl.multiple_of(y * QUART, 128), QUART)
        wgrad[r0:r0 + n, at_y] = g * (1.0 / math.sqrt(TOK * NZ * NX * NY))
        for dev in (yp, ym, y2):
            last[len(last)] = same(wgrad.at[pl.ds(r0, n), at_y], dev)

    def wout_x():
        wout(0, S1, G[z, x, 0:S1])

    def wout_y():
        gyx[2].wait_recv()
        gyx[3].wait_recv()
        wout(S1, S2, G[z, x, S1:BLK] + (yxb[0] + yxb[1]))

    def fwd(src, lo, width, at_col):
        a = A[pl.ds(pl.multiple_of(y * TOK, TOK), TOK), :]
        p = jnp.dot(a, src[:, :, :, lo:lo + width].reshape(NZ * ZBLK, width), preferred_element_type=F32)
        proj[:, pl.ds(at_col, width)] = p.astype(BF16)

    def lane(k):
        return pl.multiple_of(MAIN + yy(k) * TILE, TILE)

    def fwd_main(n):
        if n < 4:
            fwd(Wp, 256 * n, 256, 256 * n)
        else:
            fwd(Wp, MAIN, TILE, lane(0))

    def fwd_rest(n):
        fwd(Wr, n * TILE, TILE, lane((-1, 1, 2)[n]))

    def bwd(ref, cols, zi):
        wide = ref.shape[-1]
        return lax.dot_general(
            cols, ref[zi].reshape(ZBLK, wide), (((1,), (1,)), ((), ())), preferred_element_type=F32
        )

    def bwd_other(j):
        bo[j] = bwd(Wp, cotp[:, 0:WIDE], 4 * (1 - c) + j)

    def bwd_own(j):
        bm[j] = bwd(Wp, cotp[:, 0:WIDE], 4 * c + j)

    def bwd_send(j):
        bo[j] += bwd(Wr, cotp[:, WIDE:], 4 * (1 - c) + j)
        back[j] = push(bo.at[j], br.at[j], core)

    def bwd_rest(j):
        bm[j] += bwd(Wr, cotp[:, WIDE:], 4 * c + j)

    def bwd_out(j):
        back[j].wait_recv()
        igrad[:, j * ZBLK:(j + 1) * ZBLK] = (bm[j] + br[j]).astype(BF16)

    Wp[z, x, :, 0:MAIN] = w[:, 0:MAIN]
    Wp[z, x, :, MAIN:WIDE] = w[:, pl.ds(pl.multiple_of(MAIN + TILE * y, TILE), TILE)]
    barrier = pltpu.get_barrier_semaphore()
    for dev in (zp, zm, xp, xm, yp, ym, y2, core):
        pl.semaphore_signal(barrier, inc=1, device_id=dev, device_id_type=MESH)
    pl.semaphore_wait(barrier, 8)

    att(0)
    rx()
    att(1)
    zpush(1)
    rpush(1, 0)
    xpush(0)
    own()
    rx_on()
    rpush(1, -1)
    rpush(1, 1)
    zstep(1)
    xpush(-1)
    xpush(1)
    xstep(0)
    rstep(1, 0)
    cross_in(0)
    rx_in()
    rpush(1, 2)
    cots(1)
    cots(-1)
    rstep(1, -1)
    rstep(1, 1)
    xstep(-1)
    att_on(0)
    att_on(1)
    zstep(2)
    xpush(2)
    xpush(-2)
    xstep(1)
    rstep(2, 0)
    xlast(0)
    rstep(1, 2)
    xlast(-1)
    rstep(2, -1)
    cross(-1)
    cross(1)
    rstep(2, 1)
    xstep(2)
    ypush(-1)
    zstep(3)
    xpush(-3)
    cots(2)
    xpush(3)
    xstep(-2)
    rstep(3, 0)
    cross_in(-1)
    xlast(1)
    ypush(1)
    rstep(2, 2)
    xlast(2)
    ypush(2)
    rstep(3, -1)
    cross_in(1)
    rstep(3, 1)
    ypush(0)
    xstep(-3)
    zstep(4)
    xpush(4)
    cross(2)
    rstep(4, 0)
    xstep(3)
    rstep(3, 2)
    ystep(-1)
    rstep(4, -1)
    xlast(-2)
    ypush(-2)
    rstep(4, 1)
    rstep(4, 2)
    cots_in()
    xlast(-3)
    ypush(-3)
    cross_in(2)
    term(4)
    sumy(1, 2)
    sumy(1, -1)
    sumy(1, 0)
    sumx(4)
    ystep(1)
    term(-3)
    sumy(1, 1)
    ystep(2)
    term(3)
    xlast(3)
    sumx(3)
    sumy(2, 2)
    sumx(-3)
    term(-2)
    ystep(0)
    sumx_on(4)
    sumx(-2)
    sumy(2, -1)
    sumy(2, 1)
    term(2)
    sumx(2)
    ystep(-2)
    ylast(-1)
    sumx_on(-3)
    sumy(3, 2)
    sumx_on(3)
    xstep(4)
    term(1)
    sumx_in(4)
    sumz(1)
    sumy(3, -1)
    term(-1)
    ypush(3)
    sumx(1)
    sumx_on(2)
    term(0)
    ystep(-3)
    ylast(2)
    sumy(3, 1)
    sumx(0)
    sumx_in(-3)
    sumy(2, 0)
    sumx_on(-2)
    sumy(4, 2)
    sumx(-1)
    ylast(0)
    ylast(1)
    sumx_in(3)
    sumz(2)
    sumy(4, -1)
    xlast(4)
    ypush(4)
    fwd_main(1)
    sumy(4, 1)
    ystep(3)
    fwd_main(3)
    sumx_in(2)
    sumy(3, 0)
    ylast(-2)
    sumx_on(1)
    sumx_on(0)
    ylast(-3)
    bwd_other(0)
    fwd_main(4)
    ystep(4)
    sumy(5, 2)
    sumx_in(-2)
    sumyx()
    fwd_main(0)
    sumz(3)
    sumx_on(-1)
    bwd_other(2)
    ylast(3)
    sumx_in(1)
    sumy(5, -1)
    bwd_other(1)
    bwd_other(3)
    sumx_in(0)
    ylast(4)
    bwd_send(3)
    bwd_send(2)
    bwd_send(0)
    bwd_send(1)
    sumy(5, 1)
    sumyx_on()
    sumy(4, 0)
    bwd_own(3)
    bwd_rest(3)
    sumx_in(-1)
    fwd_rest(2)
    sumz(4)
    fwd_main(2)
    bwd_out(3)
    sumy(5, 0)
    wout_y()
    fwd_rest(0)
    bwd_own(2)
    bwd_rest(2)
    sumz(5)
    wout_x()
    bwd_out(2)
    bwd_own(0)
    bwd_rest(0)
    fwd_rest(1)
    bwd_out(0)
    bwd_own(1)
    bwd_rest(1)
    bwd_out(1)

    for k in sorted(last):
        last[k].wait_recv()
    for copy in started:
        copy.wait_send()


def body(attn, w, cot):
    vmem = pl.BlockSpec(memory_space=pltpu.VMEM)
    f32s = [
        (NZ, NX, BLK, QUART),
        (4, TOK, ZBLK),
        (4, TOK, ZBLK),
        (4, TOK, ZBLK),
        (NZ, 2, H1, QUART),
        (NZ, 2, S1, QUART),
        (3, 2, S1, QUART),
        (2, H1, QUART),
        (3, 2, NX, S2, QUART),
        (2, NX, H2, QUART),
        (2, H2, QUART),
        (2, S2, QUART),
    ]
    bf16s = [(NY * TOK, 2 * HALF), (NY * TOK, QUART), (NZ, NX, BLK, WIDE), (NZ, NX, BLK, HALF - WIDE), (TOK, HALF)]
    return pl.pallas_call(
        kernel,
        out_shape=(
            jax.ShapeDtypeStruct((TOK, HALF), BF16),
            jax.ShapeDtypeStruct((TOK, HALF), BF16),
            jax.ShapeDtypeStruct((BLK, HALF), F32),
        ),
        in_specs=[vmem] * 3,
        out_specs=(vmem,) * 3,
        scratch_shapes=[pltpu.VMEM(s, BF16) for s in bf16s]
        + [pltpu.VMEM(s, F32) for s in f32s]
        + [pltpu.SemaphoreType.DMA((N_MSG,)), pltpu.SemaphoreType.DMA((N_MSG,))],
        compiler_params=pltpu.CompilerParams(
            collective_id=0, has_side_effects=True, vmem_limit_bytes=56 * 2**20
        ),
        name="projection",
    )(attn, w, cot)


def solution(mesh):
    in_specs = (P(("depth", "row"), "col"), P("row", "col"), P(("depth", "row"), "col"))
    out_specs = (P(("depth", "row"), "col"), P(("depth", "row"), "col"), P("row", "col"))
    return jax.shard_map(body, mesh=mesh, in_specs=in_specs, out_specs=out_specs, check_vma=False)
```

```python
import math

import jax
import jax.numpy as jnp
from jax import lax
from jax.experimental import pallas as pl
from jax.experimental.pallas import tpu as pltpu
from jax.sharding import PartitionSpec as P

MESH = pl.DeviceIdType.MESH
NZ, NX, NY = 8, 4, 4
TOK, HALF, BLK = 256, 1536, 96
MAIN, TILE = 1024, 128
WIDE = MAIN + TILE
QUART = HALF // NY
R1 = 64
R2 = BLK - R1
S1 = 48
S2 = BLK - S1
H1, H2 = S1 // 2, S2 // 2
M2 = S1 + H2
ZBLK = NX * BLK
F32, BF16 = jnp.float32, jnp.bfloat16
N_MSG = 224


def kernel(attn, w, cot, proj, igrad, wgrad, A, CQ, Wp, Wr, Wx, cotp, cotx, pv, iv, G, bo, bm, br,
           xa, xb, za, za4, ya, yb, yxa, yxb, wv, send, recv, local):
    row, c, y = lax.axis_index("row"), lax.axis_index("col"), lax.axis_index("depth")
    z, x = row // NX, lax.rem(row, NX)

    def zz(k):
        return lax.rem(z + (k % NZ), NZ)

    def xx(k):
        return lax.rem(x + (k % NX), NX)

    def yy(k):
        return lax.rem(y + (k % NY), NY)

    zp, zm = (zz(1) * NX + x, c, y), (zz(-1) * NX + x, c, y)
    xp, xm = (z * NX + xx(1), c, y), (z * NX + xx(-1), c, y)
    yp, ym, y2 = (row, c, yy(1)), (row, c, yy(-1)), (row, c, yy(2))
    core = (row, 1 - c, y)
    started = []

    def push(src, dst, dev):
        k = len(started)
        copy = pltpu.make_async_remote_copy(
            src_ref=src, dst_ref=dst, send_sem=send.at[k], recv_sem=recv.at[k], device_id=dev, device_id_type=MESH
        )
        copy.start()
        started.append(copy)
        return copy

    def same(ref, dev):
        return push(ref, ref, dev)

    moved = []

    def move(src, dst):
        moved.append(pltpu.make_async_copy(src, dst, local.at[len(moved)]))
        moved[-1].start()

    at, ct, cc, wz, wx, wr, wxr, wy = {}, {}, {}, {}, {}, {}, {}, {}
    gx, gz, gy, gyx, last, back = {}, {}, {}, {}, {}, {}

    def four(k):
        return lax.rem(z + k, 4)

    def piece(k, p, h):
        lane0 = pl.multiple_of(h * HALF + four(k) * ZBLK, 128)
        return A.at[pl.ds(pl.multiple_of(yy(p) * TOK, TOK), TOK), pl.ds(lane0, ZBLK)]

    def att(k):
        src = attn.at[:, pl.ds(pl.multiple_of(four(k) * ZBLK, 128), ZBLK)]
        at[k, 0] = push(src, piece(k, 0, c), yp)
        at[k, 1] = push(src, piece(k, 0, c), ym)

    def att_on(k):
        side = 0 if k in (1, 4) else 1
        at[k, side].wait_recv()
        at[k, 2] = same(piece(k, 2 * side - 1, c), ym if side else yp)

    def cross(k):
        at[k, 1 if k in (1, 4) else 0].wait_recv()
        for p in (-1, 1):
            cc[k, p] = same(piece(k, p, c), core)

    def cross2(k):
        at[k, 2].wait_recv()
        cc[k, 2] = same(piece(k, 2, c), core)

    def cross_in(k):
        for p in (-1, 1, 2):
            cc[k, p].wait_recv()

    def cots(k):
        q = cot.at[:, pl.ds(pl.multiple_of(yy(k) * QUART, 128), QUART)]
        ct[k] = push(q, CQ.at[pl.ds(pl.multiple_of(y * TOK, TOK), TOK), :], {1: yp, -1: ym, 2: y2}[k])

    def cots_in():
        for k in (1, -1, 2):
            ct[k].wait_recv()

    def own():
        at_y = pl.ds(pl.multiple_of(y * TOK, TOK), TOK)
        mine = A.at[at_y, pl.ds(pl.multiple_of(c * HALF, 128), HALF)]
        cc[0] = push(attn, mine, core)
        move(attn, mine)
        move(cot.at[:, pl.ds(pl.multiple_of(y * QUART, 128), QUART)], CQ.at[at_y, :])
        move(cot.at[:, pl.ds(0, MAIN)], cotp.at[:, pl.ds(0, MAIN)])
        for j, k in enumerate((0, -1, 1, 2)):
            move(cot.at[:, pl.ds(lane(k), TILE)], cotp.at[:, pl.ds(MAIN + j * TILE, TILE)])

    def own_in():
        for copy in moved[2:9]:
            copy.wait()
        cc[0].wait_recv()
        cc[1] = push(cotp.at[:, pl.ds(WIDE, HALF - WIDE)], cotx, core)

    def blk(k, r0, n):
        return Wp.at[zz(k), x, pl.ds(r0, n), :]

    def zpush(step):
        k, h = step - 1, R1 // 2
        if step < 4:
            wz[step, 0] = same(blk(-k, 0, R1), zp)
            wz[step, 1] = same(blk(k, 0, R1), zm)
        else:
            wz[step, 0] = same(blk(-k, 0, h), zp)
            wz[step, 1] = same(blk(k, h, h), zm)

    def zstep(step):
        wz[step, 0].wait_recv()
        wz[step, 1].wait_recv()
        if step < 4:
            zpush(step + 1)

    def xpush(k):
        wx[k, 0] = same(blk(k, 0, R1), xp)
        wx[k, 1] = same(blk(k, 0, R1), xm)

    def xstep(k):
        h = R1 // 2
        wx[k, 0].wait_recv()
        wx[k, 2] = same(Wp.at[zz(k), xx(-1), pl.ds(0, h), :], xp)
        wx[k, 1].wait_recv()
        wx[k, 3] = same(Wp.at[zz(k), xx(1), pl.ds(h, h), :], xm)

    def xlast(k):
        wx[k, 2].wait_recv()
        wx[k, 3].wait_recv()

    def rx():
        mine = Wp.at[z, x, pl.ds(R1, R2), :]
        wxr[0] = same(mine, xp)
        wxr[1] = same(mine, xm)

    def rx_on():
        h = R2 // 2
        wxr[0].wait_recv()
        wxr[2] = same(Wp.at[z, xx(-1), pl.ds(R1, h), :], xp)
        wxr[1].wait_recv()
        wxr[3] = same(Wp.at[z, xx(1), pl.ds(R1 + h, h), :], xm)

    def rx_in():
        wxr[2].wait_recv()
        wxr[3].wait_recv()

    def rpush(step, j):
        k, h = step - 1, R2 // 2
        if step < 4:
            wr[step, j, 0] = same(Wp.at[zz(-k), xx(j), pl.ds(R1, R2), :], zp)
            wr[step, j, 1] = same(Wp.at[zz(k), xx(j), pl.ds(R1, R2), :], zm)
        else:
            wr[step, j, 0] = same(Wp.at[zz(-k), xx(j), pl.ds(R1, h), :], zp)
            wr[step, j, 1] = same(Wp.at[zz(k), xx(j), pl.ds(R1 + h, h), :], zm)

    def rstep(step, j):
        wr[step, j, 0].wait_recv()
        wr[step, j, 1].wait_recv()
        if step < 4:
            rpush(step + 1, j)

    def wtile(k, j):
        return Wr.at[zz(k), :, :, pl.ds(j * TILE, TILE)]

    def ypush(k):
        src = Wp.at[zz(k), :, :, pl.ds(MAIN, TILE)]
        wy[k, 0] = push(src, wtile(k, 0), yp)
        wy[k, 1] = push(src, wtile(k, 1), ym)

    def ystep(k):
        j = k % 2
        wy[k, j].wait_recv()
        wy[k, 2] = push(wtile(k, j), wtile(k, 2), ym if j else yp)

    def ylast(k):
        wy[k, 1 - k % 2].wait_recv()
        wy[k, 2].wait_recv()

    def term(k):
        @pl.loop(0, 2)
        def _(i):
            zi = lax.rem(z + k + 4 * i, NZ)
            a = A[:, pl.ds(pl.multiple_of(zi * ZBLK, 128), ZBLK)]
            g = lax.dot_general(a, CQ[...], (((0,), (0,)), ((), ())), preferred_element_type=F32)
            G[zi] = g.reshape(NX, BLK, QUART)

    def sumx(k):
        gx[k, 0] = push(G.at[zz(k), xx(2), pl.ds(0, H1)], xa.at[k % NZ, 0], xp)
        gx[k, 1] = push(G.at[zz(k), xx(2), pl.ds(H1, H1)], xa.at[k % NZ, 1], xm)

    def sumx_on(k):
        gx[k, 0].wait_recv()
        G[zz(k), xx(1), 0:H1] += xa[k % NZ, 0]
        gx[k, 2] = push(G.at[zz(k), xx(1), pl.ds(0, S1)], xb.at[k % NZ, 0], xp)
        gx[k, 1].wait_recv()
        G[zz(k), xx(-1), H1:S1] += xa[k % NZ, 1]
        gx[k, 3] = push(G.at[zz(k), xx(-1), pl.ds(0, S1)], xb.at[k % NZ, 1], xm)

    def sumx_in(k):
        gx[k, 2].wait_recv()
        gx[k, 3].wait_recv()
        G[zz(k), x, 0:S1] += xb[k % NZ, 0] + xb[k % NZ, 1]

    def sumz(step):
        if step == 1:
            gz[1, 0] = push(G.at[zz(4), x, pl.ds(0, H1)], za4.at[0], zp)
            gz[1, 1] = push(G.at[zz(4), x, pl.ds(H1, H1)], za4.at[1], zm)
            return
        gz[step - 1, 0].wait_recv()
        gz[step - 1, 1].wait_recv()
        if step == 2:
            G[zz(3), x, 0:H1] += za4[0]
            G[zz(-3), x, H1:S1] += za4[1]
        elif step < 5:
            G[zz(5 - step), x, 0:S1] += za[step - 3, 0]
            G[zz(step - 5), x, 0:S1] += za[step - 3, 1]
        else:
            G[z, x, 0:S1] += za[2, 0] + za[2, 1]
            return
        gz[step, 0] = push(G.at[zz(5 - step), x, pl.ds(0, S1)], za.at[step - 2, 0], zp)
        gz[step, 1] = push(G.at[zz(step - 5), x, pl.ds(0, S1)], za.at[step - 2, 1], zm)

    def sumy(step, j):
        i, d = xx(j), j % NX
        if step == 1:
            gy[1, j, 0] = push(G.at[zz(4), i, pl.ds(S1, H2)], yb.at[0, d], zp)
            gy[1, j, 1] = push(G.at[zz(4), i, pl.ds(M2, H2)], yb.at[1, d], zm)
            return
        gy[step - 1, j, 0].wait_recv()
        gy[step - 1, j, 1].wait_recv()
        if step == 2:
            G[zz(3), i, S1:M2] += yb[0, d]
            G[zz(-3), i, M2:BLK] += yb[1, d]
        elif step < 5:
            G[zz(5 - step), i, S1:BLK] += ya[step - 3, 0, d]
            G[zz(step - 5), i, S1:BLK] += ya[step - 3, 1, d]
        else:
            G[z, i, S1:BLK] += ya[2, 0, d] + ya[2, 1, d]
            return
        gy[step, j, 0] = push(G.at[zz(5 - step), i, pl.ds(S1, S2)], ya.at[step - 2, 0, d], zp)
        gy[step, j, 1] = push(G.at[zz(step - 5), i, pl.ds(S1, S2)], ya.at[step - 2, 1, d], zm)

    def sumyx():
        gyx[0] = push(G.at[z, xx(2), pl.ds(S1, H2)], yxa.at[0], xp)
        gyx[1] = push(G.at[z, xx(2), pl.ds(M2, H2)], yxa.at[1], xm)

    def sumyx_on():
        gyx[0].wait_recv()
        G[z, xx(1), S1:M2] += yxa[0]
        gyx[2] = push(G.at[z, xx(1), pl.ds(S1, S2)], yxb.at[0], xp)
        gyx[1].wait_recv()
        G[z, xx(-1), M2:BLK] += yxa[1]
        gyx[3] = push(G.at[z, xx(-1), pl.ds(S1, S2)], yxb.at[1], xm)

    def wout(r0, n, g):
        at_y = pl.ds(pl.multiple_of(y * QUART, 128), QUART)
        wv[r0:r0 + n, :] = g * (1.0 / math.sqrt(TOK * NZ * NX * NY))
        part = wv.at[pl.ds(r0, n), :]
        there = wgrad.at[pl.ds(r0, n), at_y]
        for dev in (yp, ym, y2):
            last[len(last)] = push(part, there, dev)
        move(part, there)

    def wout_x():
        wout(0, S1, G[z, x, 0:S1])

    def wout_y():
        gyx[2].wait_recv()
        gyx[3].wait_recv()
        wout(S1, S2, G[z, x, S1:BLK] + (yxb[0] + yxb[1]))

    def fwd(src, lo, width, at_col):
        a = A[pl.ds(pl.multiple_of(y * TOK, TOK), TOK), :]
        p = jnp.dot(a, src[:, :, :, pl.ds(lo, width)].reshape(NZ * ZBLK, width), preferred_element_type=F32)
        pv[:, pl.ds(at_col, width)] = p.astype(BF16)

    def lane(k):
        return pl.multiple_of(MAIN + yy(k) * TILE, TILE)

    def fwd_main():
        @pl.loop(0, 4)
        def _(n):
            lo = pl.multiple_of(n * 256, 256)
            fwd(Wp, lo, 256, lo)

        fwd(Wp, MAIN, TILE, lane(0))
        move(pv.at[:, pl.ds(0, MAIN)], proj.at[:, pl.ds(0, MAIN)])

    def fwd_rest():
        p = jnp.dot(A[pl.ds(pl.multiple_of(y * TOK, TOK), TOK), :], Wr[...].reshape(NZ * ZBLK, HALF - WIDE),
                    preferred_element_type=F32).astype(BF16)
        for n, k in enumerate((-1, 1, 2)):
            pv[:, pl.ds(lane(k), TILE)] = p[:, n * TILE:(n + 1) * TILE]
        move(pv.at[:, pl.ds(MAIN, HALF - MAIN)], proj.at[:, pl.ds(MAIN, HALF - MAIN)])

    def bwd(cols, panel):
        panel = panel.reshape(ZBLK, panel.shape[-1])
        return lax.dot_general(cols, panel, (((1,), (1,)), ((), ())), preferred_element_type=F32)

    def bwd_other():
        @pl.loop(0, 4)
        def _(j):
            bo[j] = bwd(cotp[:, 0:WIDE], Wp[4 * (1 - c) + j])

        back[0] = push(bo, br, core)

    def bwd_own():
        @pl.loop(0, 4)
        def _(j):
            bm[j] = bwd(cotp[:, 0:WIDE], Wp[4 * c + j])

    def bwd_in():
        back[0].wait_recv()
        cc[1].wait_recv()

    def wcross(k):
        back[k] = push(Wr.at[4 * (1 - c) + four(k)], Wx.at[four(k)], core)

    def bwd_out(k):
        back[k].wait_recv()
        j = four(k)
        cols = pl.ds(pl.multiple_of(j * ZBLK, 128), ZBLK)
        rest = bwd(cotp[:, WIDE:], Wr[4 * c + j]) + bwd(cotx[...], Wx[j])
        iv[:, cols] = (bm[j] + br[j] + rest).astype(BF16)
        move(iv.at[:, cols], igrad.at[:, cols])

    move(w.at[:, pl.ds(0, MAIN)], Wp.at[z, x, :, pl.ds(0, MAIN)])
    move(w.at[:, pl.ds(lane(0), TILE)], Wp.at[z, x, :, pl.ds(MAIN, TILE)])
    barrier = pltpu.get_barrier_semaphore()
    for dev in (zp, zm, xp, xm, yp, ym, y2, core):
        pl.semaphore_signal(barrier, inc=1, device_id=dev, device_id_type=MESH)
    pl.semaphore_wait(barrier, 8)

    def w_in():
        for copy in moved[:2]:
            copy.wait()

    w_in()
    zpush(1)
    att(4)
    own()
    rx()
    xpush(0)
    rpush(1, 0)
    att(3)
    rx_on()
    rpush(1, -1)
    rpush(1, 1)
    zstep(1)
    xpush(1)
    att(1)
    xpush(-1)
    own_in()
    rstep(1, 0)
    rx_in()
    xstep(0)
    rstep(1, -1)
    cots(2)
    rstep(1, 1)
    xstep(1)
    att_on(4)
    cross(4)
    att_on(3)
    cross(3)
    rpush(1, 2)
    zstep(2)
    xpush(-2)
    xstep(-1)
    xlast(0)
    cots(1)
    cots(-1)
    xpush(2)
    rstep(2, -1)
    xlast(1)
    rstep(2, 1)
    att_on(1)
    cross(1)
    rstep(1, 2)
    xstep(-2)
    cross2(4)
    cross2(3)
    rstep(2, 0)
    xlast(-1)
    zstep(3)
    xpush(-3)
    att(2)
    xpush(3)
    cross_in(4)
    rstep(3, -1)
    cots_in()
    term(4)
    cross_in(3)
    term(3)
    xlast(-2)
    rstep(3, 1)
    sumy(1, 2)
    rstep(2, 2)
    sumx(4)
    ypush(-2)
    xstep(2)
    sumy(1, 1)
    cross2(1)
    sumy(1, -1)
    att_on(2)
    zstep(4)
    xpush(4)
    sumy(1, 0)
    rstep(4, -1)
    ypush(1)
    rstep(3, 0)
    rstep(4, 1)
    cross_in(1)
    term(1)
    sumy(2, 2)
    ypush(-1)
    cross(2)
    xstep(3)
    rstep(3, 2)
    sumy(2, 1)
    sumx_on(4)
    xlast(2)
    ypush(2)
    sumy(2, -1)
    cross2(2)
    sumx(-3)
    ystep(-2)
    rstep(4, 0)
    xstep(-3)
    sumy(2, 0)
    ystep(1)
    sumx(3)
    cross_in(2)
    term(2)
    xlast(3)
    sumx(-2)
    ypush(3)
    xstep(4)
    sumy(3, 2)
    rstep(4, 2)
    sumy(3, 1)
    sumx_in(4)
    ystep(-1)
    ystep(2)
    sumx(2)
    sumz(1)
    sumx_on(-3)
    sumy(3, -1)
    ypush(0)
    xlast(-3)
    ylast(-2)
    sumx(1)
    sumy(3, 0)
    ylast(1)
    sumx_on(3)
    ypush(-3)
    sumy(4, 2)
    sumx_on(-2)
    xlast(4)
    bwd_other()
    ylast(2)
    ystep(3)
    sumy(4, 1)
    sumx(-1)
    ylast(-1)
    sumx_on(2)
    sumx_in(-3)
    fwd_main()
    ystep(0)
    sumx_in(3)
    sumz(2)
    sumy(4, -1)
    ypush(4)
    ystep(-3)
    sumy(5, 2)
    sumx_in(-2)
    sumyx()
    sumy(4, 0)
    sumx_on(1)
    sumx(0)
    sumx_on(-1)
    sumy(5, 1)
    wcross(2)
    bwd_own()
    sumx_in(2)
    sumz(3)
    ylast(0)
    ylast(3)
    wcross(3)
    sumy(5, -1)
    sumyx_on()
    sumx_in(1)
    ystep(4)
    bwd_in()
    sumx_on(0)
    sumy(5, 0)
    ylast(-3)
    wcross(1)
    bwd_out(2)
    sumx_in(-1)
    sumz(4)
    bwd_out(3)
    wout_y()
    ylast(4)
    wcross(4)
    fwd_rest()
    bwd_out(1)
    sumx_in(0)
    sumz(5)
    wout_x()
    bwd_out(4)

    for k in sorted(last):
        last[k].wait_recv()
    for copy in started:
        copy.wait_send()
    for copy in moved[9:]:
        copy.wait()


def pass_on(*refs):
    for i in range(3):
        refs[i + 3][...] = refs[i][...]


def body(attn, w, cot):
    whole = pl.BlockSpec(memory_space=pl.ANY)
    f32s = [
        (NZ, NX, BLK, QUART),
        (4, TOK, ZBLK),
        (4, TOK, ZBLK),
        (4, TOK, ZBLK),
        (NZ, 2, H1, QUART),
        (NZ, 2, S1, QUART),
        (3, 2, S1, QUART),
        (2, H1, QUART),
        (3, 2, NX, S2, QUART),
        (2, NX, H2, QUART),
        (2, H2, QUART),
        (2, S2, QUART),
        (BLK, QUART),
    ]
    rest = HALF - WIDE
    bf16s = [(NY * TOK, 2 * HALF), (NY * TOK, QUART), (NZ, NX, BLK, WIDE), (NZ, NX, BLK, rest), (4, NX, BLK, rest)]
    bf16s += [(TOK, HALF), (TOK, rest), (TOK, HALF), (TOK, HALF)]
    outs = tuple(pltpu.VMEM((n, HALF), t) for n, t in ((TOK, BF16), (TOK, BF16), (BLK, F32)))
    attn, w, cot = (pltpu.with_memory_space_constraint(v, pltpu.HBM) for v in (attn, w, cot))
    done = pl.pallas_call(
        kernel,
        out_shape=outs,
        in_specs=[whole] * 3,
        out_specs=(whole,) * 3,
        scratch_shapes=[pltpu.VMEM(s, BF16) for s in bf16s]
        + [pltpu.VMEM(s, F32) for s in f32s]
        + [pltpu.SemaphoreType.DMA((N_MSG,)), pltpu.SemaphoreType.DMA((N_MSG,)), pltpu.SemaphoreType.DMA((20,))],
        compiler_params=pltpu.CompilerParams(
            collective_id=0, has_side_effects=True, vmem_limit_bytes=40 * 2**20
        ),
        name="projection",
    )(attn, w, cot)
    return done


def solution(mesh):
    in_specs = (P(("depth", "row"), "col"), P("row", "col"), P(("depth", "row"), "col"))
    out_specs = (P(("depth", "row"), "col"), P(("depth", "row"), "col"), P("row", "col"))
    return jax.shard_map(body, mesh=mesh, in_specs=in_specs, out_specs=out_specs, check_vma=False)
```

```python
import math

import jax
import jax.numpy as jnp
from jax import lax
from jax.experimental import pallas as pl
from jax.experimental.pallas import tpu as pltpu
from jax.sharding import PartitionSpec as P

MESH = pl.DeviceIdType.MESH
NZ, NX, NY = 8, 4, 4
TOK, HALF, BLK = 256, 1536, 96
MAIN, TILE = 1024, 128
WIDE = MAIN + TILE
ROWS, COLS = BLK // 2, HALF // 2
R1 = 64
R2 = BLK - R1
S1 = ROWS // 2
C1 = COLS // 2
ZBLK = NX * BLK
PIECE = 2 * NX * ROWS
F32, BF16 = jnp.float32, jnp.bfloat16
N_MSG = 224


def kernel(attn, w, cot, proj, igrad, wgrad, A, AH, AO, CQ, PM, Wp, Wr, Wx, cotp, cotx, pv, iv, G, bo, bm, br,
           xa, xb, za, za4, ya, yb, yxa, yxb, wv, send, recv, local):
    row, c, y = lax.axis_index("row"), lax.axis_index("col"), lax.axis_index("depth")
    z, x = row // NX, lax.rem(row, NX)

    def zz(k):
        return lax.rem(z + (k % NZ), NZ)

    def xx(k):
        return lax.rem(x + (k % NX), NX)

    def yy(k):
        return lax.rem(y + k, NY)

    zp, zm = (zz(1) * NX + x, c, y), (zz(-1) * NX + x, c, y)
    xp, xm = (z * NX + xx(1), c, y), (z * NX + xx(-1), c, y)
    yh, yd = yy(1 - 2 * lax.rem(y, 2)), yy(3 + 2 * lax.rem(y, 2))
    my_h, my_d = y // 2, lax.rem((y + 1) // 2, 2)
    ph, pd, y2 = (row, c, yh), (row, c, yd), (row, c, yy(2))
    core = (row, 1 - c, y)
    started = []

    def push(src, dst, dev):
        k = len(started)
        copy = pltpu.make_async_remote_copy(
            src_ref=src, dst_ref=dst, send_sem=send.at[k], recv_sem=recv.at[k], device_id=dev, device_id_type=MESH
        )
        copy.start()
        started.append(copy)
        return copy

    def same(ref, dev):
        return push(ref, ref, dev)

    moved = []

    def move(src, dst):
        moved.append(pltpu.make_async_copy(src, dst, local.at[len(moved)]))
        moved[-1].start()

    at, ct, cc, wz, wx, wr, wxr, wy = {}, {}, {}, {}, {}, {}, {}, {}
    gx, gz, gy, gyx, last, back = {}, {}, {}, {}, {}, {}

    def four(k):
        return lax.rem(z + k, 4)

    def own():
        move(attn, A.at[:, pl.ds(pl.multiple_of(c * HALF, 128), HALF)])
        at_y = pl.ds(pl.multiple_of(y * TOK, TOK), TOK)
        move(cot.at[:, pl.ds(pl.multiple_of(my_d * COLS, 128), COLS)], CQ.at[at_y, :])
        move(cot.at[:, pl.ds(0, MAIN)], cotp.at[:, pl.ds(0, MAIN)])
        for j, k in enumerate((y, yh, yd, yy(2))):
            move(cot.at[:, pl.ds(lane(k), TILE)], cotp.at[:, pl.ds(MAIN + j * TILE, TILE)])

    def own_push():
        cc[0] = push(attn, A.at[:, pl.ds(pl.multiple_of(c * HALF, 128), HALF)], core)

    def own_in():
        for copy in moved[3:9]:
            copy.wait()
        cc[0].wait_recv()
        cc[1] = push(cotp.at[:, pl.ds(WIDE, HALF - WIDE)], cotx, core)

    def piece(p, who, side):
        lane0 = pl.multiple_of(side * COLS + (p - 1) * PIECE, 128)
        return AH.at[pl.ds(pl.multiple_of(who * TOK, TOK), TOK), pl.ds(lane0, PIECE)]

    def perm(p):
        if p == 1:
            moved[2].wait()
            src = lax.broadcasted_iota(jnp.int32, (ZBLK, PIECE), 0)
            dst = lax.broadcasted_iota(jnp.int32, (ZBLK, PIECE), 1)
            for second in (0, 1):
                d = dst - second * (PIECE // 2)
                ok = (d >= 0) & (d < PIECE // 2)
                for n in range(1, NX):
                    d = d + jnp.where(dst >= second * (PIECE // 2) + n * ROWS, BLK - ROWS, 0)
                for other in (0, 1):
                    half = my_h + other - 2 * my_h * other
                    PM[second, other] = jnp.where(ok & (src == d + ROWS * half), 1.0, 0.0).astype(BF16)
        ks = (4, 3) if p == 1 else (1, 2)
        cols = [A[:, pl.ds(pl.multiple_of(c * HALF + four(k) * ZBLK, 128), ZBLK)] for k in ks]
        for other in (0, 1):
            g = sum(jnp.dot(cols[n], PM[n, other], preferred_element_type=F32) for n in (0, 1)).astype(BF16)
            if other:
                AO[p - 1] = g
            else:
                lane0 = pl.multiple_of(c * COLS + (p - 1) * PIECE, 128)
                AH[pl.ds(pl.multiple_of(y * TOK, TOK), TOK), pl.ds(lane0, PIECE)] = g

    def att(p):
        at[p, 0] = same(piece(p, y, c), ph)
        at[p, 1] = push(AO.at[p - 1], piece(p, y, c), pd)
        cc[p, 0] = same(piece(p, y, c), core)

    def att_on(p):
        at[p, 1].wait_recv()
        at[p, 2] = same(piece(p, yd, c), ph)
        cc[p, 1] = same(piece(p, yd, c), core)

    def cross(p):
        at[p, 0].wait_recv()
        cc[p, 2] = same(piece(p, yh, c), core)

    def cross2(p):
        at[p, 2].wait_recv()
        cc[p, 3] = same(piece(p, yy(2), c), core)

    def cross_in(p):
        for i in range(4):
            cc[p, i].wait_recv()

    def crow(who):
        return CQ.at[pl.ds(pl.multiple_of(who * TOK, TOK), TOK), :]

    def cots():
        ct[0] = push(cot.at[:, pl.ds(pl.multiple_of((1 - my_d) * COLS, 128), COLS)], crow(y), ph)
        ct[1] = push(cot.at[:, pl.ds(pl.multiple_of(my_d * COLS, 128), COLS)], crow(y), pd)

    def cots_on():
        ct[0].wait_recv()
        ct[2] = same(crow(yh), pd)

    def cots_in():
        ct[1].wait_recv()
        ct[2].wait_recv()

    def blk(k, r0, n):
        return Wp.at[zz(k), x, pl.ds(r0, n), :]

    def zpush(step):
        k, h = step - 1, R1 // 2
        if step < 4:
            wz[step, 0] = same(blk(-k, 0, R1), zp)
            wz[step, 1] = same(blk(k, 0, R1), zm)
        else:
            wz[step, 0] = same(blk(-k, 0, h), zp)
            wz[step, 1] = same(blk(k, h, h), zm)

    def zstep(step):
        wz[step, 0].wait_recv()
        wz[step, 1].wait_recv()
        if step < 4:
            zpush(step + 1)

    def xpush(k):
        wx[k, 0] = same(blk(k, 0, R1), xp)
        wx[k, 1] = same(blk(k, 0, R1), xm)

    def xstep(k):
        h = R1 // 2
        wx[k, 0].wait_recv()
        wx[k, 2] = same(Wp.at[zz(k), xx(-1), pl.ds(0, h), :], xp)
        wx[k, 1].wait_recv()
        wx[k, 3] = same(Wp.at[zz(k), xx(1), pl.ds(h, h), :], xm)

    def xlast(k):
        wx[k, 2].wait_recv()
        wx[k, 3].wait_recv()

    def rx():
        mine = Wp.at[z, x, pl.ds(R1, R2), :]
        wxr[0] = same(mine, xp)
        wxr[1] = same(mine, xm)

    def rx_on():
        h = R2 // 2
        wxr[0].wait_recv()
        wxr[2] = same(Wp.at[z, xx(-1), pl.ds(R1, h), :], xp)
        wxr[1].wait_recv()
        wxr[3] = same(Wp.at[z, xx(1), pl.ds(R1 + h, h), :], xm)

    def rx_in():
        wxr[2].wait_recv()
        wxr[3].wait_recv()

    def rpush(step, j):
        k, h = step - 1, R2 // 2
        if step < 4:
            wr[step, j, 0] = same(Wp.at[zz(-k), xx(j), pl.ds(R1, R2), :], zp)
            wr[step, j, 1] = same(Wp.at[zz(k), xx(j), pl.ds(R1, R2), :], zm)
        else:
            wr[step, j, 0] = same(Wp.at[zz(-k), xx(j), pl.ds(R1, h), :], zp)
            wr[step, j, 1] = same(Wp.at[zz(k), xx(j), pl.ds(R1 + h, h), :], zm)

    def rstep(step, j):
        wr[step, j, 0].wait_recv()
        wr[step, j, 1].wait_recv()
        if step < 4:
            rpush(step + 1, j)

    def wtile(k, j):
        return Wr.at[zz(k), :, :, pl.ds(j * TILE, TILE)]

    def ypush(k):
        src = Wp.at[zz(k), :, :, pl.ds(MAIN, TILE)]
        wy[k, 0] = push(src, wtile(k, 0), ph)
        wy[k, 1] = push(src, wtile(k, 1), pd)

    def ystep(k):
        j = k % 2
        wy[k, j].wait_recv()
        wy[k, 2] = push(wtile(k, j), wtile(k, 2), ph if j else pd)

    def ylast(k):
        wy[k, 1 - k % 2].wait_recv()
        wy[k, 2].wait_recv()

    def term(p):
        ka, kb = (4, 3) if p == 1 else (1, 2)

        @pl.loop(0, 2)
        def _(i):
            a = AH[:, pl.ds(pl.multiple_of(i * COLS + (p - 1) * PIECE, 128), PIECE)]
            g = lax.dot_general(a, CQ[...], (((0,), (0,)), ((), ())), preferred_element_type=F32)
            g = g.reshape(2, NX, ROWS, COLS)
            G[4 * i + four(ka)] = g[0]
            G[4 * i + four(kb)] = g[1]

    lo, hi = pl.ds(0, C1), pl.ds(C1, C1)
    ra, rb = pl.ds(0, S1), pl.ds(S1, S1)

    def sumx(k):
        gx[k, 0] = push(G.at[zz(k), xx(2), ra, lo], xa.at[k % NZ, 0], xp)
        gx[k, 1] = push(G.at[zz(k), xx(2), ra, hi], xa.at[k % NZ, 1], xm)

    def sumx_on(k):
        gx[k, 0].wait_recv()
        G[zz(k), xx(1), 0:S1, 0:C1] += xa[k % NZ, 0]
        gx[k, 2] = push(G.at[zz(k), xx(1), ra], xb.at[k % NZ, 0], xp)
        gx[k, 1].wait_recv()
        G[zz(k), xx(-1), 0:S1, C1:] += xa[k % NZ, 1]
        gx[k, 3] = push(G.at[zz(k), xx(-1), ra], xb.at[k % NZ, 1], xm)

    def sumx_in(k):
        gx[k, 2].wait_recv()
        gx[k, 3].wait_recv()
        G[zz(k), x, 0:S1] += xb[k % NZ, 0] + xb[k % NZ, 1]

    def sumz(step):
        if step == 1:
            gz[1, 0] = push(G.at[zz(4), x, ra, lo], za4.at[0], zp)
            gz[1, 1] = push(G.at[zz(4), x, ra, hi], za4.at[1], zm)
            return
        gz[step - 1, 0].wait_recv()
        gz[step - 1, 1].wait_recv()
        if step == 2:
            G[zz(3), x, 0:S1, 0:C1] += za4[0]
            G[zz(-3), x, 0:S1, C1:] += za4[1]
        elif step < 5:
            G[zz(5 - step), x, 0:S1] += za[step - 3, 0]
            G[zz(step - 5), x, 0:S1] += za[step - 3, 1]
        else:
            G[z, x, 0:S1] += za[2, 0] + za[2, 1]
            return
        gz[step, 0] = push(G.at[zz(5 - step), x, ra], za.at[step - 2, 0], zp)
        gz[step, 1] = push(G.at[zz(step - 5), x, ra], za.at[step - 2, 1], zm)

    def sumy(step, j):
        i, d = xx(j), j % NX
        if step == 1:
            gy[1, j, 0] = push(G.at[zz(4), i, rb, lo], yb.at[0, d], zp)
            gy[1, j, 1] = push(G.at[zz(4), i, rb, hi], yb.at[1, d], zm)
            return
        gy[step - 1, j, 0].wait_recv()
        gy[step - 1, j, 1].wait_recv()
        if step == 2:
            G[zz(3), i, S1:, 0:C1] += yb[0, d]
            G[zz(-3), i, S1:, C1:] += yb[1, d]
        elif step < 5:
            G[zz(5 - step), i, S1:] += ya[step - 3, 0, d]
            G[zz(step - 5), i, S1:] += ya[step - 3, 1, d]
        else:
            G[z, i, S1:] += ya[2, 0, d] + ya[2, 1, d]
            return
        gy[step, j, 0] = push(G.at[zz(5 - step), i, rb], ya.at[step - 2, 0, d], zp)
        gy[step, j, 1] = push(G.at[zz(step - 5), i, rb], ya.at[step - 2, 1, d], zm)

    def sumyx():
        gyx[0] = push(G.at[z, xx(2), rb, lo], yxa.at[0], xp)
        gyx[1] = push(G.at[z, xx(2), rb, hi], yxa.at[1], xm)

    def sumyx_on():
        gyx[0].wait_recv()
        G[z, xx(1), S1:, 0:C1] += yxa[0]
        gyx[2] = push(G.at[z, xx(1), rb], yxb.at[0], xp)
        gyx[1].wait_recv()
        G[z, xx(-1), S1:, C1:] += yxa[1]
        gyx[3] = push(G.at[z, xx(-1), rb], yxb.at[1], xm)

    def wout(r0, g):
        wv[r0:r0 + S1, :] = g * (1.0 / math.sqrt(TOK * NZ * NX * NY))
        part = wv.at[pl.ds(r0, S1), :]
        there = wgrad.at[pl.ds(pl.multiple_of(my_h * ROWS + r0, 8), S1), pl.ds(pl.multiple_of(my_d * COLS, 128), COLS)]
        for dev in (ph, pd, y2):
            last[len(last)] = push(part, there, dev)
        move(part, there)

    def wout_x():
        wout(0, G[z, x, 0:S1])

    def wout_y():
        gyx[2].wait_recv()
        gyx[3].wait_recv()
        wout(S1, G[z, x, S1:] + (yxb[0] + yxb[1]))

    def fwd(src, lane0, width, at_col):
        p = jnp.dot(A[...], src[:, :, :, pl.ds(lane0, width)].reshape(NZ * ZBLK, width), preferred_element_type=F32)
        pv[:, pl.ds(at_col, width)] = p.astype(BF16)

    def lane(who):
        return pl.multiple_of(MAIN + who * TILE, TILE)

    def fwd_main():
        @pl.loop(0, 4)
        def _(n):
            lane0 = pl.multiple_of(n * 256, 256)
            fwd(Wp, lane0, 256, lane0)

        fwd(Wp, MAIN, TILE, lane(y))
        move(pv.at[:, pl.ds(0, MAIN)], proj.at[:, pl.ds(0, MAIN)])

    def fwd_rest():
        p = jnp.dot(A[...], Wr[...].reshape(NZ * ZBLK, HALF - WIDE),
                    preferred_element_type=F32).astype(BF16)
        for n, k in enumerate((yh, yd, yy(2))):
            pv[:, pl.ds(lane(k), TILE)] = p[:, n * TILE:(n + 1) * TILE]
        move(pv.at[:, pl.ds(MAIN, HALF - MAIN)], proj.at[:, pl.ds(MAIN, HALF - MAIN)])

    def bwd(cols, panel):
        panel = panel.reshape(ZBLK, panel.shape[-1])
        return lax.dot_general(cols, panel, (((1,), (1,)), ((), ())), preferred_element_type=F32)

    def bwd_other():
        @pl.loop(0, 4)
        def _(j):
            bo[j] = bwd(cotp[:, 0:WIDE], Wp[4 * (1 - c) + j])

        back[0] = push(bo, br, core)

    def bwd_own():
        @pl.loop(0, 4)
        def _(j):
            bm[j] = bwd(cotp[:, 0:WIDE], Wp[4 * c + j])

    def bwd_in():
        back[0].wait_recv()
        cc[1].wait_recv()

    def wcross(k):
        back[k] = push(Wr.at[4 * (1 - c) + four(k)], Wx.at[four(k)], core)

    def bwd_out(k):
        back[k].wait_recv()
        j = four(k)
        cols = pl.ds(pl.multiple_of(j * ZBLK, 128), ZBLK)
        rest = bwd(cotp[:, WIDE:], Wr[4 * c + j]) + bwd(cotx[...], Wx[j])
        iv[:, cols] = (bm[j] + br[j] + rest).astype(BF16)
        move(iv.at[:, cols], igrad.at[:, cols])

    move(w.at[:, pl.ds(0, MAIN)], Wp.at[z, x, :, pl.ds(0, MAIN)])
    move(w.at[:, pl.ds(lane(y), TILE)], Wp.at[z, x, :, pl.ds(MAIN, TILE)])
    barrier = pltpu.get_barrier_semaphore()
    for dev in (zp, zm, xp, xm, ph, pd, y2, core):
        pl.semaphore_signal(barrier, inc=1, device_id=dev, device_id_type=MESH)
    pl.semaphore_wait(barrier, 8)

    def w_in():
        for copy in moved[:2]:
            copy.wait()

    cots()
    w_in()
    rx()
    zpush(1)
    xpush(0)
    rpush(1, 0)
    own()
    own_push()
    perm(1)
    perm(2)
    rx_on()
    rpush(1, 1)
    rpush(1, -1)
    own_in()
    att(1)
    zstep(1)
    xpush(-1)
    xpush(1)
    rx_in()
    rpush(1, 2)
    xstep(0)
    att(2)
    rstep(1, -1)
    xstep(-1)
    rstep(1, 1)
    cots_on()
    zstep(2)
    xstep(1)
    att_on(1)
    cross(1)
    xpush(-2)
    xlast(0)
    rstep(1, 2)
    xlast(-1)
    xpush(2)
    cross(2)
    att_on(2)
    rstep(2, 1)
    xlast(1)
    rstep(1, 0)
    zstep(3)
    ypush(-1)
    xstep(-2)
    xpush(-3)
    cross2(1)
    rstep(2, 2)
    ypush(0)
    cross_in(1)
    rstep(3, 1)
    xstep(2)
    rstep(2, -1)
    ypush(1)
    cots_in()
    term(1)
    sumy(1, 2)
    sumy(1, 1)
    sumx(4)
    ystep(-1)
    cross2(2)
    xpush(3)
    sumy(1, -1)
    zstep(4)
    xlast(-2)
    rstep(3, 2)
    rstep(4, 1)
    ystep(0)
    xpush(4)
    rstep(2, 0)
    ypush(-2)
    cross_in(2)
    xlast(2)
    term(2)
    ypush(2)
    sumy(2, 2)
    xstep(-3)
    sumy(2, 1)
    ystep(1)
    ylast(0)
    ylast(-1)
    rstep(4, 2)
    xstep(3)
    rstep(3, -1)
    sumy(2, -1)
    ystep(-2)
    sumx_on(4)
    rstep(3, 0)
    xstep(4)
    ystep(2)
    sumy(3, 2)
    xlast(-3)
    ypush(-3)
    sumx(-1)
    sumy(3, 1)
    ylast(-2)
    rstep(4, -1)
    ylast(1)
    sumx(3)
    xlast(3)
    ypush(3)
    sumx(-2)
    sumy(1, 0)
    sumx(-3)
    sumy(3, -1)
    sumx_in(4)
    ylast(2)
    wcross(2)
    rstep(4, 0)
    sumx(1)
    sumx(2)
    sumz(1)
    xlast(4)
    ypush(4)
    fwd_main()
    sumy(4, 2)
    sumx_on(3)
    ystep(3)
    sumy(4, 1)
    sumx_on(-3)
    sumy(2, 0)
    sumx_on(-2)
    ystep(-3)
    bwd_own()
    sumx_on(2)
    sumy(4, -1)
    ystep(4)
    bwd_other()
    sumx_in(3)
    sumy(5, 2)
    sumyx()
    sumx_in(-3)
    sumz(2)
    sumy(5, 1)
    sumx(0)
    sumx_on(1)
    ylast(3)
    wcross(3)
    ylast(-3)
    wcross(1)
    sumx_in(-2)
    sumy(3, 0)
    ylast(4)
    wcross(4)
    fwd_rest()
    sumx_on(-1)
    sumy(5, -1)
    sumx_in(2)
    sumyx_on()
    sumz(3)
    bwd_in()
    bwd_out(2)
    sumx_on(0)
    bwd_out(3)
    sumy(4, 0)
    sumx_in(1)
    bwd_out(1)
    bwd_out(4)
    sumx_in(-1)
    sumz(4)
    sumy(5, 0)
    wout_y()
    sumx_in(0)
    sumz(5)
    wout_x()

    for k in sorted(last):
        last[k].wait_recv()
    for copy in started:
        copy.wait_send()
    for copy in moved[9:]:
        copy.wait()


def pass_on(*refs):
    for i in range(3):
        refs[i + 3][...] = refs[i][...]


def body(attn, w, cot):
    whole = pl.BlockSpec(memory_space=pl.ANY)
    f32s = [
        (NZ, NX, ROWS, COLS),
        (4, TOK, ZBLK),
        (4, TOK, ZBLK),
        (4, TOK, ZBLK),
        (NZ, 2, S1, C1),
        (NZ, 2, S1, COLS),
        (3, 2, S1, COLS),
        (2, S1, C1),
        (3, 2, NX, S1, COLS),
        (2, NX, S1, C1),
        (2, S1, C1),
        (2, S1, COLS),
        (ROWS, COLS),
    ]
    rest = HALF - WIDE
    bf16s = [(TOK, 2 * HALF), (NY * TOK, HALF), (2, TOK, PIECE), (NY * TOK, COLS), (2, 2, ZBLK, PIECE)]
    bf16s += [(NZ, NX, BLK, WIDE), (NZ, NX, BLK, rest), (4, NX, BLK, rest)]
    bf16s += [(TOK, HALF), (TOK, rest), (TOK, HALF), (TOK, HALF)]
    outs = tuple(pltpu.VMEM((n, HALF), t) for n, t in ((TOK, BF16), (TOK, BF16), (BLK, F32)))
    attn, w, cot = (pltpu.with_memory_space_constraint(v, pltpu.HBM) for v in (attn, w, cot))
    done = pl.pallas_call(
        kernel,
        out_shape=outs,
        in_specs=[whole] * 3,
        out_specs=(whole,) * 3,
        scratch_shapes=[pltpu.VMEM(s, BF16) for s in bf16s]
        + [pltpu.VMEM(s, F32) for s in f32s]
        + [pltpu.SemaphoreType.DMA((N_MSG,)), pltpu.SemaphoreType.DMA((N_MSG,)), pltpu.SemaphoreType.DMA((20,))],
        compiler_params=pltpu.CompilerParams(
            collective_id=0, has_side_effects=True, vmem_limit_bytes=40 * 2**20
        ),
        name="projection",
    )(attn, w, cot)
    return done


def solution(mesh):
    in_specs = (P(("depth", "row"), "col"), P("row", "col"), P(("depth", "row"), "col"))
    out_specs = (P(("depth", "row"), "col"), P(("depth", "row"), "col"), P("row", "col"))
    return jax.shard_map(body, mesh=mesh, in_specs=in_specs, out_specs=out_specs, check_vma=False)
```

```python
import math

import jax
import jax.numpy as jnp
from jax import lax
from jax.experimental import pallas as pl
from jax.experimental.pallas import tpu as pltpu
from jax.sharding import PartitionSpec as P

MESH = pl.DeviceIdType.MESH
NZ, NX, NY = 8, 4, 4
TOK, HALF, BLK = 256, 1536, 96
MAIN, TILE = 1024, 128
WIDE = MAIN + TILE
ROWS, COLS = BLK // 2, HALF // 2
R1 = 64
R2 = BLK - R1
S1 = ROWS // 2
C1 = COLS // 2
CODE = S1 + S1 // 3
ZBLK = NX * BLK
PIECE = 2 * NX * ROWS
F32, BF16 = jnp.float32, jnp.bfloat16
N_MSG = 224


def kernel(attn, w, cot, proj, igrad, wgrad, A, AH, AO, CQ, PM, Wp, Wr, Wx, cotp, cotx, pv, iv, G, bo, bm, br,
           xa, xb, za, za4, ya, yb, yxa, yxb, xe, xh, ze, ye, yxe, wv, send, recv, local):
    row, c, y = lax.axis_index("row"), lax.axis_index("col"), lax.axis_index("depth")
    z, x = row // NX, lax.rem(row, NX)

    def zz(k):
        return lax.rem(z + (k % NZ), NZ)

    def xx(k):
        return lax.rem(x + (k % NX), NX)

    def yy(k):
        return lax.rem(y + k, NY)

    zp, zm = (zz(1) * NX + x, c, y), (zz(-1) * NX + x, c, y)
    xp, xm = (z * NX + xx(1), c, y), (z * NX + xx(-1), c, y)
    yh, yd = yy(1 - 2 * lax.rem(y, 2)), yy(3 + 2 * lax.rem(y, 2))
    my_h, my_d = y // 2, lax.rem((y + 1) // 2, 2)
    ph, pd, y2 = (row, c, yh), (row, c, yd), (row, c, yy(2))
    core = (row, 1 - c, y)
    started = []

    def push(src, dst, dev):
        k = len(started)
        copy = pltpu.make_async_remote_copy(
            src_ref=src, dst_ref=dst, send_sem=send.at[k], recv_sem=recv.at[k], device_id=dev, device_id_type=MESH
        )
        copy.start()
        started.append(copy)
        return copy

    def same(ref, dev):
        return push(ref, ref, dev)

    moved = []

    def move(src, dst):
        moved.append(pltpu.make_async_copy(src, dst, local.at[len(moved)]))
        moved[-1].start()

    at, ct, cc, wz, wx, wr, wxr, wy = {}, {}, {}, {}, {}, {}, {}, {}
    gx, gz, gy, gyx, last, back = {}, {}, {}, {}, {}, {}

    def four(k):
        return lax.rem(z + k, 4)

    def own():
        move(attn, A.at[:, pl.ds(pl.multiple_of(c * HALF, 128), HALF)])
        at_y = pl.ds(pl.multiple_of(y * TOK, TOK), TOK)
        move(cot.at[:, pl.ds(pl.multiple_of(my_d * COLS, 128), COLS)], CQ.at[at_y, :])
        move(cot.at[:, pl.ds(0, MAIN)], cotp.at[:, pl.ds(0, MAIN)])
        for j, k in enumerate((y, yh, yd, yy(2))):
            move(cot.at[:, pl.ds(lane(k), TILE)], cotp.at[:, pl.ds(MAIN + j * TILE, TILE)])

    def own_push():
        cc[0] = push(attn, A.at[:, pl.ds(pl.multiple_of(c * HALF, 128), HALF)], core)

    def own_in():
        for copy in moved[3:9]:
            copy.wait()
        cc[0].wait_recv()
        cc[1] = push(cotp.at[:, pl.ds(WIDE, HALF - WIDE)], cotx, core)

    def piece(p, who, side):
        lane0 = pl.multiple_of(side * COLS + (p - 1) * PIECE, 128)
        return AH.at[pl.ds(pl.multiple_of(who * TOK, TOK), TOK), pl.ds(lane0, PIECE)]

    def perm(p):
        if p == 1:
            moved[2].wait()
            src = lax.broadcasted_iota(jnp.int32, (ZBLK, PIECE), 0)
            dst = lax.broadcasted_iota(jnp.int32, (ZBLK, PIECE), 1)
            for second in (0, 1):
                d = dst - second * (PIECE // 2)
                ok = (d >= 0) & (d < PIECE // 2)
                for n in range(1, NX):
                    d = d + jnp.where(dst >= second * (PIECE // 2) + n * ROWS, BLK - ROWS, 0)
                for other in (0, 1):
                    half = my_h + other - 2 * my_h * other
                    PM[second, other] = jnp.where(ok & (src == d + ROWS * half), 1.0, 0.0).astype(BF16)
        ks = (4, 3) if p == 1 else (1, 2)
        cols = [A[:, pl.ds(pl.multiple_of(c * HALF + four(k) * ZBLK, 128), ZBLK)] for k in ks]
        for other in (0, 1):
            g = sum(jnp.dot(cols[n], PM[n, other], preferred_element_type=F32) for n in (0, 1)).astype(BF16)
            if other:
                AO[p - 1] = g
            else:
                lane0 = pl.multiple_of(c * COLS + (p - 1) * PIECE, 128)
                AH[pl.ds(pl.multiple_of(y * TOK, TOK), TOK), pl.ds(lane0, PIECE)] = g

    def att(p):
        at[p, 0] = same(piece(p, y, c), ph)
        at[p, 1] = push(AO.at[p - 1], piece(p, y, c), pd)
        cc[p, 0] = same(piece(p, y, c), core)

    def att_on(p):
        at[p, 1].wait_recv()
        at[p, 2] = same(piece(p, yd, c), ph)
        cc[p, 1] = same(piece(p, yd, c), core)

    def cross(p):
        at[p, 0].wait_recv()
        cc[p, 2] = same(piece(p, yh, c), core)

    def cross2(p):
        at[p, 2].wait_recv()
        cc[p, 3] = same(piece(p, yy(2), c), core)

    def cross_in(p):
        for i in range(4):
            cc[p, i].wait_recv()

    def crow(who):
        return CQ.at[pl.ds(pl.multiple_of(who * TOK, TOK), TOK), :]

    def cots():
        ct[0] = push(cot.at[:, pl.ds(pl.multiple_of((1 - my_d) * COLS, 128), COLS)], crow(y), ph)
        ct[1] = push(cot.at[:, pl.ds(pl.multiple_of(my_d * COLS, 128), COLS)], crow(y), pd)

    def cots_on():
        ct[0].wait_recv()
        ct[2] = same(crow(yh), pd)

    def cots_in():
        ct[1].wait_recv()
        ct[2].wait_recv()

    def blk(k, r0, n):
        return Wp.at[zz(k), x, pl.ds(r0, n), :]

    def zpush(step):
        k, h = step - 1, R1 // 2
        if step < 4:
            wz[step, 0] = same(blk(-k, 0, R1), zp)
            wz[step, 1] = same(blk(k, 0, R1), zm)
        else:
            wz[step, 0] = same(blk(-k, 0, h), zp)
            wz[step, 1] = same(blk(k, h, h), zm)

    def zstep(step):
        wz[step, 0].wait_recv()
        wz[step, 1].wait_recv()
        if step < 4:
            zpush(step + 1)

    def xpush(k):
        wx[k, 0] = same(blk(k, 0, R1), xp)
        wx[k, 1] = same(blk(k, 0, R1), xm)

    def xstep(k):
        h = R1 // 2
        wx[k, 0].wait_recv()
        wx[k, 2] = same(Wp.at[zz(k), xx(-1), pl.ds(0, h), :], xp)
        wx[k, 1].wait_recv()
        wx[k, 3] = same(Wp.at[zz(k), xx(1), pl.ds(h, h), :], xm)

    def xlast(k):
        wx[k, 2].wait_recv()
        wx[k, 3].wait_recv()

    def rx():
        mine = Wp.at[z, x, pl.ds(R1, R2), :]
        wxr[0] = same(mine, xp)
        wxr[1] = same(mine, xm)

    def rx_on():
        h = R2 // 2
        wxr[0].wait_recv()
        wxr[2] = same(Wp.at[z, xx(-1), pl.ds(R1, h), :], xp)
        wxr[1].wait_recv()
        wxr[3] = same(Wp.at[z, xx(1), pl.ds(R1 + h, h), :], xm)

    def rx_in():
        wxr[2].wait_recv()
        wxr[3].wait_recv()

    def rpush(step, j):
        k, h = step - 1, R2 // 2
        if step < 4:
            wr[step, j, 0] = same(Wp.at[zz(-k), xx(j), pl.ds(R1, R2), :], zp)
            wr[step, j, 1] = same(Wp.at[zz(k), xx(j), pl.ds(R1, R2), :], zm)
        else:
            wr[step, j, 0] = same(Wp.at[zz(-k), xx(j), pl.ds(R1, h), :], zp)
            wr[step, j, 1] = same(Wp.at[zz(k), xx(j), pl.ds(R1 + h, h), :], zm)

    def rstep(step, j):
        wr[step, j, 0].wait_recv()
        wr[step, j, 1].wait_recv()
        if step < 4:
            rpush(step + 1, j)

    def wtile(k, j):
        return Wr.at[zz(k), :, :, pl.ds(j * TILE, TILE)]

    def ypush(k):
        src = Wp.at[zz(k), :, :, pl.ds(MAIN, TILE)]
        wy[k, 0] = push(src, wtile(k, 0), ph)
        wy[k, 1] = push(src, wtile(k, 1), pd)

    def ystep(k):
        j = k % 2
        wy[k, j].wait_recv()
        wy[k, 2] = push(wtile(k, j), wtile(k, 2), ph if j else pd)

    def ylast(k):
        wy[k, 1 - k % 2].wait_recv()
        wy[k, 2].wait_recv()

    def term(p):
        ka, kb = (4, 3) if p == 1 else (1, 2)

        @pl.loop(0, 2)
        def _(i):
            a = AH[:, pl.ds(pl.multiple_of(i * COLS + (p - 1) * PIECE, 128), PIECE)]
            g = lax.dot_general(a, CQ[...], (((0,), (0,)), ((), ())), preferred_element_type=F32)
            g = g.reshape(2, NX, ROWS, COLS)
            G[4 * i + four(ka)] = g[0]
            G[4 * i + four(kb)] = g[1]

    def chunks(ref, of):
        wide = min(ref.shape[-1], 384)

        @pl.loop(0, ref.shape[-1] // wide)
        def _(i):
            of(pl.ds(pl.multiple_of(i * wide, wide), wide))

    def last_place(top):
        top = jnp.abs(top)
        return (top * (1.0 + 1.02 * 2.0**-8)).astype(BF16).astype(F32) - top

    def encode(v):
        top = v.astype(BF16).astype(F32)
        unit = jnp.maximum(last_place(top), 1e-30)
        q = jnp.clip(jnp.floor((v - top) * pl.reciprocal(unit, approx=True) * 5.0 + 0.5), -2.0, 2.0)
        n = S1 // 3
        low = q[0:n] * 25.0 + q[n:2 * n] * 5.0 + q[2 * n:]
        return jnp.concatenate([top, low], axis=0).astype(BF16)

    def decode(e):
        e = e.astype(F32)
        top, low = e[0:S1], e[S1:]
        q0 = jnp.floor((low + 12.5) * (1.0 / 25.0))
        low = low - 25.0 * q0
        q1 = jnp.floor((low + 2.5) * (1.0 / 5.0))
        q = jnp.concatenate([q0, q1, low - 5.0 * q1], axis=0)
        return top + last_place(top) * (q * 0.2)

    def collect(dst, *arrived):
        def add(cols):
            dst[:, cols] += sum(decode(a[:, cols]) for a in arrived)

        chunks(dst, add)

    lo, hi = pl.ds(0, C1), pl.ds(C1, C1)
    ra, rb = pl.ds(0, S1), pl.ds(S1, S1)

    def onward(g, arrived, out, there, dev):
        def one(cols):
            out[:, cols] = encode(g[:, cols] if arrived is None else g[:, cols] + decode(arrived[:, cols]))

        chunks(out, one)
        return push(out, there, dev)

    def sumx(k):
        n = k % NZ
        gx[k, 0] = onward(G.at[zz(k), xx(2), ra, lo], None, xh.at[n, 0], xa.at[n, 0], xp)
        gx[k, 1] = onward(G.at[zz(k), xx(2), ra, hi], None, xh.at[n, 1], xa.at[n, 1], xm)

    def sumx_on(k):
        n = k % NZ
        gx[k, 0].wait_recv()
        collect(G.at[zz(k), xx(1), ra, lo], xa.at[n, 0])
        gx[k, 2] = onward(G.at[zz(k), xx(1), ra], None, xe.at[n, 0], xb.at[n, 0], xp)
        gx[k, 1].wait_recv()
        collect(G.at[zz(k), xx(-1), ra, hi], xa.at[n, 1])
        gx[k, 3] = onward(G.at[zz(k), xx(-1), ra], None, xe.at[n, 1], xb.at[n, 1], xm)

    def sumx_in(k):
        gx[k, 2].wait_recv()
        gx[k, 3].wait_recv()
        collect(G.at[zz(k), x, ra], xb.at[k % NZ, 0], xb.at[k % NZ, 1])

    def sumz(step):
        if step == 1:
            gz[1, 0] = push(G.at[zz(4), x, ra, lo], za4.at[0], zp)
            gz[1, 1] = push(G.at[zz(4), x, ra, hi], za4.at[1], zm)
            return
        gz[step - 1, 0].wait_recv()
        gz[step - 1, 1].wait_recv()
        if step == 5:
            collect(G.at[z, x, ra], za.at[2, 0], za.at[2, 1])
            return
        if step == 2:
            G[zz(3), x, 0:S1, 0:C1] += za4[0]
            G[zz(-3), x, 0:S1, C1:] += za4[1]
        for i, dev in ((0, zp), (1, zm)):
            g = G.at[zz((5 - step) * (1 - 2 * i)), x, ra]
            gz[step, i] = onward(g, None if step == 2 else za.at[step - 3, i], ze.at[step - 2, i], za.at[step - 2, i], dev)

    def sumy(step, j):
        n, d = xx(j), j % NX
        if step == 1:
            gy[1, j, 0] = push(G.at[zz(4), n, rb, lo], yb.at[0, d], zp)
            gy[1, j, 1] = push(G.at[zz(4), n, rb, hi], yb.at[1, d], zm)
            return
        gy[step - 1, j, 0].wait_recv()
        gy[step - 1, j, 1].wait_recv()
        if step == 5:
            collect(G.at[z, n, rb], ya.at[2, 0, d], ya.at[2, 1, d])
            return
        if step == 2:
            G[zz(3), n, S1:, 0:C1] += yb[0, d]
            G[zz(-3), n, S1:, C1:] += yb[1, d]
        for i, dev in ((0, zp), (1, zm)):
            g = G.at[zz((5 - step) * (1 - 2 * i)), n, rb]
            gy[step, j, i] = onward(
                g, None if step == 2 else ya.at[step - 3, i, d], ye.at[step - 2, i, d], ya.at[step - 2, i, d], dev
            )

    def sumyx():
        gyx[0] = push(G.at[z, xx(2), rb, lo], yxa.at[0], xp)
        gyx[1] = push(G.at[z, xx(2), rb, hi], yxa.at[1], xm)

    def sumyx_on():
        gyx[0].wait_recv()
        G[z, xx(1), S1:, 0:C1] += yxa[0]
        gyx[2] = onward(G.at[z, xx(1), rb], None, yxe.at[0], yxb.at[0], xp)
        gyx[1].wait_recv()
        G[z, xx(-1), S1:, C1:] += yxa[1]
        gyx[3] = onward(G.at[z, xx(-1), rb], None, yxe.at[1], yxb.at[1], xm)

    def wout(r0, g):
        wv[r0:r0 + S1, :] = g * (1.0 / math.sqrt(TOK * NZ * NX * NY))
        part = wv.at[pl.ds(r0, S1), :]
        there = wgrad.at[pl.ds(pl.multiple_of(my_h * ROWS + r0, 8), S1), pl.ds(pl.multiple_of(my_d * COLS, 128), COLS)]
        for dev in (ph, pd, y2):
            last[len(last)] = push(part, there, dev)
        move(part, there)

    def wout_x():
        wout(0, G[z, x, 0:S1])

    def wout_y():
        gyx[2].wait_recv()
        gyx[3].wait_recv()
        wout(S1, G[z, x, S1:] + (decode(yxb[0]) + decode(yxb[1])))

    def fwd(src, lane0, width, at_col):
        p = jnp.dot(A[...], src[:, :, :, pl.ds(lane0, width)].reshape(NZ * ZBLK, width), preferred_element_type=F32)
        pv[:, pl.ds(at_col, width)] = p.astype(BF16)

    def lane(who):
        return pl.multiple_of(MAIN + who * TILE, TILE)

    def fwd_main():
        @pl.loop(0, 4)
        def _(n):
            lane0 = pl.multiple_of(n * 256, 256)
            fwd(Wp, lane0, 256, lane0)

        fwd(Wp, MAIN, TILE, lane(y))
        move(pv.at[:, pl.ds(0, MAIN)], proj.at[:, pl.ds(0, MAIN)])

    def fwd_rest():
        p = jnp.dot(A[...], Wr[...].reshape(NZ * ZBLK, HALF - WIDE),
                    preferred_element_type=F32).astype(BF16)
        for n, k in enumerate((yh, yd, yy(2))):
            pv[:, pl.ds(lane(k), TILE)] = p[:, n * TILE:(n + 1) * TILE]
        move(pv.at[:, pl.ds(MAIN, HALF - MAIN)], proj.at[:, pl.ds(MAIN, HALF - MAIN)])

    def bwd(cols, panel):
        panel = panel.reshape(ZBLK, panel.shape[-1])
        return lax.dot_general(cols, panel, (((1,), (1,)), ((), ())), preferred_element_type=F32)

    def bwd_other():
        @pl.loop(0, 4)
        def _(j):
            bo[j] = bwd(cotp[:, 0:WIDE], Wp[4 * (1 - c) + j])

        back[0] = push(bo, br, core)

    def bwd_own():
        @pl.loop(0, 4)
        def _(j):
            bm[j] = bwd(cotp[:, 0:WIDE], Wp[4 * c + j])

    def bwd_in():
        back[0].wait_recv()
        cc[1].wait_recv()

    def wcross(k):
        back[k] = push(Wr.at[4 * (1 - c) + four(k)], Wx.at[four(k)], core)

    def bwd_out(k):
        back[k].wait_recv()
        j = four(k)
        cols = pl.ds(pl.multiple_of(j * ZBLK, 128), ZBLK)
        rest = bwd(cotp[:, WIDE:], Wr[4 * c + j]) + bwd(cotx[...], Wx[j])
        iv[:, cols] = (bm[j] + br[j] + rest).astype(BF16)
        move(iv.at[:, cols], igrad.at[:, cols])

    move(w.at[:, pl.ds(0, MAIN)], Wp.at[z, x, :, pl.ds(0, MAIN)])
    move(w.at[:, pl.ds(lane(y), TILE)], Wp.at[z, x, :, pl.ds(MAIN, TILE)])
    barrier = pltpu.get_barrier_semaphore()
    for dev in (zp, zm, xp, xm, ph, pd, y2, core):
        pl.semaphore_signal(barrier, inc=1, device_id=dev, device_id_type=MESH)
    pl.semaphore_wait(barrier, 8)

    def w_in():
        for copy in moved[:2]:
            copy.wait()

    cots()
    own()
    w_in()
    rx()
    zpush(1)
    xpush(0)
    own_push()
    rpush(1, 0)
    perm(1)
    perm(2)
    rx_on()
    rpush(1, 1)
    rpush(1, -1)
    own_in()
    att(1)
    zstep(1)
    xpush(-1)
    xpush(1)
    rx_in()
    rstep(1, 0)
    att(2)
    xstep(0)
    rpush(1, 2)
    xstep(-1)
    rstep(1, -1)
    cots_on()
    cross(1)
    zstep(2)
    att_on(1)
    xpush(2)
    xlast(0)
    xpush(-2)
    rstep(1, 1)
    xlast(-1)
    cross(2)
    att_on(2)
    rstep(2, -1)
    xstep(1)
    rstep(1, 2)
    xstep(2)
    rstep(2, 0)
    ypush(0)
    cross2(1)
    xstep(-2)
    rstep(2, 1)
    ypush(-1)
    cross_in(1)
    xlast(1)
    zstep(3)
    xpush(-3)
    cots_in()
    ypush(1)
    term(1)
    cross2(2)
    ystep(0)
    sumy(1, 1)
    sumy(1, 2)
    sumx(4)
    xpush(3)
    sumy(1, -1)
    sumy(1, 0)
    xlast(2)
    xlast(-2)
    rstep(2, 2)
    ypush(-2)
    cross_in(2)
    term(2)
    xstep(-3)
    ypush(2)
    sumy(2, 2)
    sumx(2)
    sumx(3)
    sumx(-3)
    rstep(3, 0)
    ystep(1)
    sumx(-2)
    ystep(-2)
    rstep(3, 1)
    sumx_on(4)
    zstep(4)
    sumy(2, 1)
    sumy(2, -1)
    xpush(4)
    ystep(-1)
    ylast(0)
    xlast(-3)
    ystep(2)
    rstep(3, 2)
    sumy(3, 2)
    rstep(4, 0)
    ylast(1)
    sumy(2, 0)
    sumx_on(-3)
    rstep(4, 1)
    rstep(3, -1)
    ypush(-3)
    sumx_on(3)
    sumx_in(4)
    sumz(1)
    ylast(-2)
    ylast(-1)
    xstep(3)
    sumy(3, 1)
    rstep(4, 2)
    sumy(3, -1)
    sumx_on(2)
    ylast(2)
    wcross(2)
    sumy(4, 2)
    xstep(4)
    sumx_in(-3)
    ystep(-3)
    rstep(4, -1)
    sumy(3, 0)
    sumx_in(3)
    sumx(1)
    sumz(2)
    sumx(-1)
    sumx(0)
    xlast(3)
    ypush(3)
    sumy(4, 1)
    sumx_on(-2)
    sumx_in(2)
    sumy(4, -1)
    ylast(-3)
    wcross(1)
    sumy(5, 2)
    sumyx()
    xlast(4)
    ypush(4)
    bwd_other()
    sumx_on(-1)
    sumy(4, 0)
    ystep(3)
    sumx_on(1)
    sumx_in(-2)
    sumz(3)
    sumy(5, 1)
    sumy(5, -1)
    sumyx_on()
    sumx_on(0)
    ystep(4)
    bwd_own()
    sumx_in(-1)
    sumx_in(1)
    sumz(4)
    sumy(5, 0)
    wout_y()
    fwd_main()
    sumx_in(0)
    sumz(5)
    wout_x()
    ylast(4)
    wcross(4)
    ylast(3)
    wcross(3)
    fwd_rest()
    bwd_in()
    bwd_out(1)
    bwd_out(2)
    bwd_out(4)
    bwd_out(3)

    for k in sorted(last):
        last[k].wait_recv()
    for copy in started:
        copy.wait_send()
    for copy in moved[9:]:
        copy.wait()


def pass_on(*refs):
    copies = [pltpu.make_async_copy(refs[i], refs[i + 3], refs[6].at[i]) for i in range(3)]
    for i in range(3):
        copies[i].start()
    for i in range(3):
        copies[i].wait()


def body(attn, w, cot):
    whole = pl.BlockSpec(memory_space=pl.ANY)
    sums = [
        (NZ, NX, ROWS, COLS),
        (4, TOK, ZBLK),
        (4, TOK, ZBLK),
        (4, TOK, ZBLK),
        (NZ, 2, CODE, C1),
        (NZ, 2, CODE, COLS),
        (3, 2, CODE, COLS),
        (2, S1, C1),
        (3, 2, NX, CODE, COLS),
        (2, NX, S1, C1),
        (2, S1, C1),
        (2, CODE, COLS),
        (NZ, 2, CODE, COLS),
        (NZ, 2, CODE, C1),
        (3, 2, CODE, COLS),
        (3, 2, NX, CODE, COLS),
        (2, CODE, COLS),
        (ROWS, COLS),
    ]
    rest = HALF - WIDE
    bf16s = [(TOK, 2 * HALF), (NY * TOK, HALF), (2, TOK, PIECE), (NY * TOK, COLS), (2, 2, ZBLK, PIECE)]
    bf16s += [(NZ, NX, BLK, WIDE), (NZ, NX, BLK, rest), (4, NX, BLK, rest)]
    bf16s += [(TOK, HALF), (TOK, rest), (TOK, HALF), (TOK, HALF)]
    outs = tuple(pltpu.VMEM((n, HALF), t) for n, t in ((TOK, BF16), (TOK, BF16), (BLK, F32)))
    attn, w, cot = (pltpu.with_memory_space_constraint(v, pltpu.HBM) for v in (attn, w, cot))
    done = pl.pallas_call(
        kernel,
        out_shape=outs,
        in_specs=[whole] * 3,
        out_specs=(whole,) * 3,
        scratch_shapes=[pltpu.VMEM(s, BF16) for s in bf16s]
        + [pltpu.VMEM(s, BF16 if s[-2] == CODE else F32) for s in sums]
        + [pltpu.SemaphoreType.DMA((N_MSG,)), pltpu.SemaphoreType.DMA((N_MSG,)), pltpu.SemaphoreType.DMA((20,))],
        compiler_params=pltpu.CompilerParams(
            collective_id=0, has_side_effects=True, vmem_limit_bytes=40 * 2**20
        ),
        name="projection",
    )(attn, w, cot)
    return pl.pallas_call(
        pass_on,
        out_shape=[jax.ShapeDtypeStruct(o.shape, o.dtype) for o in done],
        in_specs=[whole] * 3,
        out_specs=[whole] * 3,
        scratch_shapes=[pltpu.SemaphoreType.DMA((3,))],
        name="results",
    )(*(pltpu.with_memory_space_constraint(o, pltpu.VMEM) for o in done))


def solution(mesh):
    in_specs = (P(("depth", "row"), "col"), P("row", "col"), P(("depth", "row"), "col"))
    out_specs = (P(("depth", "row"), "col"), P(("depth", "row"), "col"), P("row", "col"))
    return jax.shard_map(body, mesh=mesh, in_specs=in_specs, out_specs=out_specs, check_vma=False)
```

```python
import math

import jax
import jax.numpy as jnp
from jax import lax
from jax.experimental import pallas as pl
from jax.experimental.pallas import tpu as pltpu
from jax.sharding import PartitionSpec as P

MESH = pl.DeviceIdType.MESH
NZ, NX, NY = 8, 4, 4
TOK, HALF, BLK = 256, 1536, 96
MAIN, TILE = 1024, 128
WIDE = MAIN + TILE
ROWS, COLS = BLK // 2, HALF // 2
R1 = 64
R2 = BLK - R1
S1 = ROWS // 2
C1 = COLS // 2
CODE = S1 + S1 // 3
ZBLK = NX * BLK
PIECE = 2 * NX * ROWS
F32, BF16 = jnp.float32, jnp.bfloat16
N_MSG = 224


def kernel(attn, w, cot, proj, igrad, wgrad, A, AH, AO, CQ, PM, Wp, Wr, Wx, cotp, cotx, pv, iv, G, bo, bm, br,
           xa, xb, za, za4, ya, yb, yxa, yxb, xe, xh, ze, ye, yxe, wv, send, recv, local):
    row, c, y = lax.axis_index("row"), lax.axis_index("col"), lax.axis_index("depth")
    z, x = row // NX, lax.rem(row, NX)

    def zz(k):
        return lax.rem(z + (k % NZ), NZ)

    def xx(k):
        return lax.rem(x + (k % NX), NX)

    def yy(k):
        return lax.rem(y + k, NY)

    zp, zm = (zz(1) * NX + x, c, y), (zz(-1) * NX + x, c, y)
    xp, xm = (z * NX + xx(1), c, y), (z * NX + xx(-1), c, y)
    yh, yd = yy(1 - 2 * lax.rem(y, 2)), yy(3 + 2 * lax.rem(y, 2))
    my_h, my_d = y // 2, lax.rem((y + 1) // 2, 2)
    ph, pd, y2 = (row, c, yh), (row, c, yd), (row, c, yy(2))
    core = (row, 1 - c, y)
    started = []

    def push(src, dst, dev):
        k = len(started)
        copy = pltpu.make_async_remote_copy(
            src_ref=src, dst_ref=dst, send_sem=send.at[k], recv_sem=recv.at[k], device_id=dev, device_id_type=MESH
        )
        copy.start()
        started.append(copy)
        return copy

    def same(ref, dev):
        return push(ref, ref, dev)

    moved = []

    def move(src, dst):
        moved.append(pltpu.make_async_copy(src, dst, local.at[len(moved)]))
        moved[-1].start()

    at, ct, cc, wz, wx, wr, wxr, wy = {}, {}, {}, {}, {}, {}, {}, {}
    gx, gz, gy, gyx, last, back = {}, {}, {}, {}, {}, {}

    def four(k):
        return lax.rem(z + k, 4)

    def own():
        move(attn, A.at[:, pl.ds(pl.multiple_of(c * HALF, 128), HALF)])
        at_y = pl.ds(pl.multiple_of(y * TOK, TOK), TOK)
        move(cot.at[:, pl.ds(pl.multiple_of(my_d * COLS, 128), COLS)], CQ.at[at_y, :])
        move(cot.at[:, pl.ds(0, MAIN)], cotp.at[:, pl.ds(0, MAIN)])
        for j, k in enumerate((y, yh, yd, yy(2))):
            move(cot.at[:, pl.ds(lane(k), TILE)], cotp.at[:, pl.ds(MAIN + j * TILE, TILE)])

    def own_push():
        cc[0] = push(attn, A.at[:, pl.ds(pl.multiple_of(c * HALF, 128), HALF)], core)

    def own_in():
        for copy in moved[3:9]:
            copy.wait()
        cc[0].wait_recv()
        cc[1] = push(cotp.at[:, pl.ds(WIDE, HALF - WIDE)], cotx, core)

    def piece(p, who, side):
        lane0 = pl.multiple_of(side * COLS + (p - 1) * PIECE, 128)
        return AH.at[pl.ds(pl.multiple_of(who * TOK, TOK), TOK), pl.ds(lane0, PIECE)]

    def perm(p):
        if p == 1:
            moved[2].wait()
            src = lax.broadcasted_iota(jnp.int32, (ZBLK, PIECE), 0)
            dst = lax.broadcasted_iota(jnp.int32, (ZBLK, PIECE), 1)
            for second in (0, 1):
                d = dst - second * (PIECE // 2)
                ok = (d >= 0) & (d < PIECE // 2)
                for n in range(1, NX):
                    d = d + jnp.where(dst >= second * (PIECE // 2) + n * ROWS, BLK - ROWS, 0)
                for other in (0, 1):
                    half = my_h + other - 2 * my_h * other
                    PM[second, other] = jnp.where(ok & (src == d + ROWS * half), 1.0, 0.0).astype(BF16)
        ks = (4, 3) if p == 1 else (1, 2)
        cols = [A[:, pl.ds(pl.multiple_of(c * HALF + four(k) * ZBLK, 128), ZBLK)] for k in ks]
        for other in (0, 1):
            g = sum(jnp.dot(cols[n], PM[n, other], preferred_element_type=F32) for n in (0, 1)).astype(BF16)
            if other:
                AO[p - 1] = g
            else:
                lane0 = pl.multiple_of(c * COLS + (p - 1) * PIECE, 128)
                AH[pl.ds(pl.multiple_of(y * TOK, TOK), TOK), pl.ds(lane0, PIECE)] = g

    def att(p):
        at[p, 0] = same(piece(p, y, c), ph)
        at[p, 1] = push(AO.at[p - 1], piece(p, y, c), pd)
        cc[p, 0] = same(piece(p, y, c), core)

    def att_on(p):
        at[p, 1].wait_recv()
        at[p, 2] = same(piece(p, yd, c), ph)
        cc[p, 1] = same(piece(p, yd, c), core)

    def cross(p):
        at[p, 0].wait_recv()
        cc[p, 2] = same(piece(p, yh, c), core)

    def cross2(p):
        at[p, 2].wait_recv()
        cc[p, 3] = same(piece(p, yy(2), c), core)

    def cross_in(p):
        for i in range(4):
            cc[p, i].wait_recv()

    def crow(who):
        return CQ.at[pl.ds(pl.multiple_of(who * TOK, TOK), TOK), :]

    def cots():
        ct[0] = push(cot.at[:, pl.ds(pl.multiple_of((1 - my_d) * COLS, 128), COLS)], crow(y), ph)
        ct[1] = push(cot.at[:, pl.ds(pl.multiple_of(my_d * COLS, 128), COLS)], crow(y), pd)

    def cots_on():
        ct[0].wait_recv()
        ct[2] = same(crow(yh), pd)

    def cots_in():
        ct[1].wait_recv()
        ct[2].wait_recv()

    def blk(k, r0, n):
        return Wp.at[zz(k), x, pl.ds(r0, n), :]

    def zpush(step):
        k, h = step - 1, R1 // 2
        if step < 4:
            wz[step, 0] = same(blk(-k, 0, R1), zp)
            wz[step, 1] = same(blk(k, 0, R1), zm)
        else:
            wz[step, 0] = same(blk(-k, 0, h), zp)
            wz[step, 1] = same(blk(k, h, h), zm)

    def zstep(step):
        wz[step, 0].wait_recv()
        wz[step, 1].wait_recv()
        if step < 4:
            zpush(step + 1)

    def xpush(k):
        wx[k, 0] = same(blk(k, 0, R1), xp)
        wx[k, 1] = same(blk(k, 0, R1), xm)

    def xstep(k):
        h = R1 // 2
        wx[k, 0].wait_recv()
        wx[k, 2] = same(Wp.at[zz(k), xx(-1), pl.ds(0, h), :], xp)
        wx[k, 1].wait_recv()
        wx[k, 3] = same(Wp.at[zz(k), xx(1), pl.ds(h, h), :], xm)

    def xlast(k):
        wx[k, 2].wait_recv()
        wx[k, 3].wait_recv()

    def rx():
        mine = Wp.at[z, x, pl.ds(R1, R2), :]
        wxr[0] = same(mine, xp)
        wxr[1] = same(mine, xm)

    def rx_on():
        h = R2 // 2
        wxr[0].wait_recv()
        wxr[2] = same(Wp.at[z, xx(-1), pl.ds(R1, h), :], xp)
        wxr[1].wait_recv()
        wxr[3] = same(Wp.at[z, xx(1), pl.ds(R1 + h, h), :], xm)

    def rx_in():
        wxr[2].wait_recv()
        wxr[3].wait_recv()

    def rpush(step, j):
        k, h = step - 1, R2 // 2
        if step < 4:
            wr[step, j, 0] = same(Wp.at[zz(-k), xx(j), pl.ds(R1, R2), :], zp)
            wr[step, j, 1] = same(Wp.at[zz(k), xx(j), pl.ds(R1, R2), :], zm)
        else:
            wr[step, j, 0] = same(Wp.at[zz(-k), xx(j), pl.ds(R1, h), :], zp)
            wr[step, j, 1] = same(Wp.at[zz(k), xx(j), pl.ds(R1 + h, h), :], zm)

    def rstep(step, j):
        wr[step, j, 0].wait_recv()
        wr[step, j, 1].wait_recv()
        if step < 4:
            rpush(step + 1, j)

    def wtile(k, j):
        return Wr.at[zz(k), :, :, pl.ds(j * TILE, TILE)]

    def ypush(k):
        src = Wp.at[zz(k), :, :, pl.ds(MAIN, TILE)]
        wy[k, 0] = push(src, wtile(k, 0), ph)
        wy[k, 1] = push(src, wtile(k, 1), pd)

    def ystep(k):
        j = k % 2
        wy[k, j].wait_recv()
        wy[k, 2] = push(wtile(k, j), wtile(k, 2), ph if j else pd)

    def ylast(k):
        wy[k, 1 - k % 2].wait_recv()
        wy[k, 2].wait_recv()

    def term(p):
        ka, kb = (4, 3) if p == 1 else (1, 2)

        @pl.loop(0, 2)
        def _(i):
            a = AH[:, pl.ds(pl.multiple_of(i * COLS + (p - 1) * PIECE, 128), PIECE)]
            g = lax.dot_general(a, CQ[...], (((0,), (0,)), ((), ())), preferred_element_type=F32)
            g = g.reshape(2, NX, ROWS, COLS)
            G[4 * i + four(ka)] = g[0]
            G[4 * i + four(kb)] = g[1]

    def chunks(ref, of):
        wide = min(ref.shape[-1], 384)

        @pl.loop(0, ref.shape[-1] // wide)
        def _(i):
            of(pl.ds(pl.multiple_of(i * wide, wide), wide))

    def last_place(top):
        top = jnp.abs(top)
        return (top * (1.0 + 1.02 * 2.0**-8)).astype(BF16).astype(F32) - top

    def encode(v):
        top = v.astype(BF16).astype(F32)
        unit = jnp.maximum(last_place(top), 1e-30)
        q = jnp.clip(jnp.floor((v - top) * pl.reciprocal(unit, approx=True) * 5.0 + 0.5), -2.0, 2.0)
        n = S1 // 3
        low = q[0:n] * 25.0 + q[n:2 * n] * 5.0 + q[2 * n:]
        return jnp.concatenate([top, low], axis=0).astype(BF16)

    def decode(e):
        e = e.astype(F32)
        top, low = e[0:S1], e[S1:]
        q0 = jnp.floor((low + 12.5) * (1.0 / 25.0))
        low = low - 25.0 * q0
        q1 = jnp.floor((low + 2.5) * (1.0 / 5.0))
        q = jnp.concatenate([q0, q1, low - 5.0 * q1], axis=0)
        return top + last_place(top) * (q * 0.2)

    def collect(dst, *arrived):
        def add(cols):
            dst[:, cols] += sum(decode(a[:, cols]) for a in arrived)

        chunks(dst, add)

    lo, hi = pl.ds(0, C1), pl.ds(C1, C1)
    ra, rb = pl.ds(0, S1), pl.ds(S1, S1)

    def onward(g, arrived, out, there, dev):
        def one(cols):
            out[:, cols] = encode(g[:, cols] if arrived is None else g[:, cols] + decode(arrived[:, cols]))

        chunks(out, one)
        return push(out, there, dev)

    def sumx(k):
        n = k % NZ
        gx[k, 0] = onward(G.at[zz(k), xx(2), ra, lo], None, xh.at[n, 0], xa.at[n, 0], xp)
        gx[k, 1] = onward(G.at[zz(k), xx(2), ra, hi], None, xh.at[n, 1], xa.at[n, 1], xm)

    def sumx_on(k):
        n = k % NZ
        gx[k, 0].wait_recv()
        collect(G.at[zz(k), xx(1), ra, lo], xa.at[n, 0])
        gx[k, 2] = onward(G.at[zz(k), xx(1), ra], None, xe.at[n, 0], xb.at[n, 0], xp)
        gx[k, 1].wait_recv()
        collect(G.at[zz(k), xx(-1), ra, hi], xa.at[n, 1])
        gx[k, 3] = onward(G.at[zz(k), xx(-1), ra], None, xe.at[n, 1], xb.at[n, 1], xm)

    def sumx_in(k):
        gx[k, 2].wait_recv()
        gx[k, 3].wait_recv()
        collect(G.at[zz(k), x, ra], xb.at[k % NZ, 0], xb.at[k % NZ, 1])

    def sumz(step):
        if step == 1:
            gz[1, 0] = push(G.at[zz(4), x, ra, lo], za4.at[0], zp)
            gz[1, 1] = push(G.at[zz(4), x, ra, hi], za4.at[1], zm)
            return
        gz[step - 1, 0].wait_recv()
        gz[step - 1, 1].wait_recv()
        if step == 5:
            collect(G.at[z, x, ra], za.at[2, 0], za.at[2, 1])
            return
        if step == 2:
            G[zz(3), x, 0:S1, 0:C1] += za4[0]
            G[zz(-3), x, 0:S1, C1:] += za4[1]
        for i, dev in ((0, zp), (1, zm)):
            g = G.at[zz((5 - step) * (1 - 2 * i)), x, ra]
            gz[step, i] = onward(g, None if step == 2 else za.at[step - 3, i], ze.at[step - 2, i], za.at[step - 2, i], dev)

    def sumy(step, j):
        n, d = xx(j), j % NX
        if step == 1:
            gy[1, j, 0] = push(G.at[zz(4), n, rb, lo], yb.at[0, d], zp)
            gy[1, j, 1] = push(G.at[zz(4), n, rb, hi], yb.at[1, d], zm)
            return
        gy[step - 1, j, 0].wait_recv()
        gy[step - 1, j, 1].wait_recv()
        if step == 5:
            collect(G.at[z, n, rb], ya.at[2, 0, d], ya.at[2, 1, d])
            return
        if step == 2:
            G[zz(3), n, S1:, 0:C1] += yb[0, d]
            G[zz(-3), n, S1:, C1:] += yb[1, d]
        for i, dev in ((0, zp), (1, zm)):
            g = G.at[zz((5 - step) * (1 - 2 * i)), n, rb]
            gy[step, j, i] = onward(
                g, None if step == 2 else ya.at[step - 3, i, d], ye.at[step - 2, i, d], ya.at[step - 2, i, d], dev
            )

    def sumyx():
        gyx[0] = push(G.at[z, xx(2), rb, lo], yxa.at[0], xp)
        gyx[1] = push(G.at[z, xx(2), rb, hi], yxa.at[1], xm)

    def sumyx_on():
        gyx[0].wait_recv()
        G[z, xx(1), S1:, 0:C1] += yxa[0]
        gyx[2] = onward(G.at[z, xx(1), rb], None, yxe.at[0], yxb.at[0], xp)
        gyx[1].wait_recv()
        G[z, xx(-1), S1:, C1:] += yxa[1]
        gyx[3] = onward(G.at[z, xx(-1), rb], None, yxe.at[1], yxb.at[1], xm)

    def wout(r0, g):
        wv[r0:r0 + S1, :] = g * (1.0 / math.sqrt(TOK * NZ * NX * NY))
        part = wv.at[pl.ds(r0, S1), :]
        there = wgrad.at[pl.ds(pl.multiple_of(my_h * ROWS + r0, 8), S1), pl.ds(pl.multiple_of(my_d * COLS, 128), COLS)]
        for dev in (ph, pd, y2):
            last[len(last)] = push(part, there, dev)
        move(part, there)

    def wout_x():
        wout(0, G[z, x, 0:S1])

    def wout_y():
        gyx[2].wait_recv()
        gyx[3].wait_recv()
        wout(S1, G[z, x, S1:] + (decode(yxb[0]) + decode(yxb[1])))

    def fwd(src, lane0, width, at_col):
        p = jnp.dot(A[...], src[:, :, :, pl.ds(lane0, width)].reshape(NZ * ZBLK, width), preferred_element_type=F32)
        pv[:, pl.ds(at_col, width)] = p.astype(BF16)

    def lane(who):
        return pl.multiple_of(MAIN + who * TILE, TILE)

    def fwd_main():
        @pl.loop(0, 4)
        def _(n):
            lane0 = pl.multiple_of(n * 256, 256)
            fwd(Wp, lane0, 256, lane0)

        fwd(Wp, MAIN, TILE, lane(y))
        move(pv.at[:, pl.ds(0, MAIN)], proj.at[:, pl.ds(0, MAIN)])

    def fwd_rest():
        p = jnp.dot(A[...], Wr[...].reshape(NZ * ZBLK, HALF - WIDE),
                    preferred_element_type=F32).astype(BF16)
        for n, k in enumerate((yh, yd, yy(2))):
            pv[:, pl.ds(lane(k), TILE)] = p[:, n * TILE:(n + 1) * TILE]
        move(pv.at[:, pl.ds(MAIN, HALF - MAIN)], proj.at[:, pl.ds(MAIN, HALF - MAIN)])

    def bwd(cols, panel):
        panel = panel.reshape(ZBLK, panel.shape[-1])
        return lax.dot_general(cols, panel, (((1,), (1,)), ((), ())), preferred_element_type=F32)

    def bwd_other():
        @pl.loop(0, 4)
        def _(j):
            bo[j] = bwd(cotp[:, 0:WIDE], Wp[4 * (1 - c) + j])

        back[0] = push(bo, br, core)

    def bwd_own():
        @pl.loop(0, 4)
        def _(j):
            bm[j] = bwd(cotp[:, 0:WIDE], Wp[4 * c + j])

    def bwd_in():
        back[0].wait_recv()
        cc[1].wait_recv()

    def wcross(k):
        back[k] = push(Wr.at[4 * (1 - c) + four(k)], Wx.at[four(k)], core)

    def bwd_out(k):
        back[k].wait_recv()
        j = four(k)
        cols = pl.ds(pl.multiple_of(j * ZBLK, 128), ZBLK)
        rest = bwd(cotp[:, WIDE:], Wr[4 * c + j]) + bwd(cotx[...], Wx[j])
        iv[:, cols] = (bm[j] + br[j] + rest).astype(BF16)
        move(iv.at[:, cols], igrad.at[:, cols])

    move(w.at[:, pl.ds(0, MAIN)], Wp.at[z, x, :, pl.ds(0, MAIN)])
    move(w.at[:, pl.ds(lane(y), TILE)], Wp.at[z, x, :, pl.ds(MAIN, TILE)])
    barrier = pltpu.get_barrier_semaphore()
    for dev in (zp, zm, xp, xm, ph, pd, y2, core):
        pl.semaphore_signal(barrier, inc=1, device_id=dev, device_id_type=MESH)
    pl.semaphore_wait(barrier, 8)

    def w_in():
        for copy in moved[:2]:
            copy.wait()

    cots()
    own()
    w_in()
    rx()
    zpush(1)
    xpush(0)
    own_push()
    rpush(1, 0)
    perm(1)
    perm(2)
    rx_on()
    rpush(1, 1)
    rpush(1, -1)
    own_in()
    att(1)
    zstep(1)
    xpush(-1)
    xpush(1)
    rx_in()
    rstep(1, 0)
    att(2)
    xstep(0)
    rpush(1, 2)
    xstep(-1)
    rstep(1, -1)
    cots_on()
    cross(1)
    zstep(2)
    att_on(1)
    xpush(2)
    xlast(0)
    xpush(-2)
    rstep(1, 1)
    xlast(-1)
    cross(2)
    att_on(2)
    rstep(2, -1)
    xstep(1)
    rstep(1, 2)
    xstep(2)
    rstep(2, 0)
    ypush(0)
    cross2(1)
    xstep(-2)
    rstep(2, 1)
    ypush(-1)
    cross_in(1)
    xlast(1)
    zstep(3)
    xpush(-3)
    cots_in()
    ypush(1)
    term(1)
    cross2(2)
    ystep(0)
    sumy(1, 1)
    sumy(1, 2)
    sumx(4)
    xpush(3)
    sumy(1, -1)
    sumy(1, 0)
    xlast(2)
    xlast(-2)
    rstep(2, 2)
    ypush(-2)
    cross_in(2)
    term(2)
    xstep(-3)
    ypush(2)
    sumy(2, 2)
    sumx(2)
    sumx(3)
    sumx(-3)
    rstep(3, 0)
    ystep(1)
    sumx(-2)
    ystep(-2)
    rstep(3, 1)
    sumx_on(4)
    zstep(4)
    sumy(2, 1)
    sumy(2, -1)
    xpush(4)
    ystep(-1)
    ylast(0)
    xlast(-3)
    ystep(2)
    rstep(3, 2)
    sumy(3, 2)
    rstep(4, 0)
    ylast(1)
    sumy(2, 0)
    sumx_on(-3)
    rstep(4, 1)
    rstep(3, -1)
    ypush(-3)
    sumx_on(3)
    sumx_in(4)
    sumz(1)
    ylast(-2)
    ylast(-1)
    xstep(3)
    sumy(3, 1)
    rstep(4, 2)
    sumy(3, -1)
    sumx_on(2)
    ylast(2)
    wcross(2)
    sumy(4, 2)
    xstep(4)
    sumx_in(-3)
    ystep(-3)
    rstep(4, -1)
    sumy(3, 0)
    sumx_in(3)
    sumx(1)
    sumz(2)
    sumx(-1)
    sumx(0)
    xlast(3)
    ypush(3)
    sumy(4, 1)
    sumx_on(-2)
    sumx_in(2)
    sumy(4, -1)
    ylast(-3)
    wcross(1)
    sumy(5, 2)
    sumyx()
    xlast(4)
    ypush(4)
    bwd_other()
    sumx_on(-1)
    sumy(4, 0)
    ystep(3)
    sumx_on(1)
    sumx_in(-2)
    sumz(3)
    sumy(5, 1)
    sumy(5, -1)
    sumyx_on()
    sumx_on(0)
    ystep(4)
    sumx_in(-1)
    sumx_in(1)
    sumz(4)
    sumy(5, 0)
    wout_y()
    fwd_main()
    sumx_in(0)
    sumz(5)
    wout_x()
    ylast(4)
    wcross(4)
    ylast(3)
    wcross(3)
    bwd_own()
    fwd_rest()
    bwd_in()
    bwd_out(1)
    bwd_out(2)
    bwd_out(4)
    bwd_out(3)

    for k in sorted(last):
        last[k].wait_recv()
    for copy in started:
        copy.wait_send()
    for copy in moved[9:]:
        copy.wait()


def pass_on(*refs):
    copies = [pltpu.make_async_copy(refs[i], refs[i + 3], refs[6].at[i]) for i in range(3)]
    for i in range(3):
        copies[i].start()
    for i in range(3):
        copies[i].wait()


def body(attn, w, cot):
    whole = pl.BlockSpec(memory_space=pl.ANY)
    sums = [
        (NZ, NX, ROWS, COLS),
        (4, TOK, ZBLK),
        (4, TOK, ZBLK),
        (4, TOK, ZBLK),
        (NZ, 2, CODE, C1),
        (NZ, 2, CODE, COLS),
        (3, 2, CODE, COLS),
        (2, S1, C1),
        (3, 2, NX, CODE, COLS),
        (2, NX, S1, C1),
        (2, S1, C1),
        (2, CODE, COLS),
        (NZ, 2, CODE, COLS),
        (NZ, 2, CODE, C1),
        (3, 2, CODE, COLS),
        (3, 2, NX, CODE, COLS),
        (2, CODE, COLS),
        (ROWS, COLS),
    ]
    rest = HALF - WIDE
    bf16s = [(TOK, 2 * HALF), (NY * TOK, HALF), (2, TOK, PIECE), (NY * TOK, COLS), (2, 2, ZBLK, PIECE)]
    bf16s += [(NZ, NX, BLK, WIDE), (NZ, NX, BLK, rest), (4, NX, BLK, rest)]
    bf16s += [(TOK, HALF), (TOK, rest), (TOK, HALF), (TOK, HALF)]
    outs = tuple(pltpu.VMEM((n, HALF), t) for n, t in ((TOK, BF16), (TOK, BF16), (BLK, F32)))
    attn, w, cot = (pltpu.with_memory_space_constraint(v, pltpu.HBM) for v in (attn, w, cot))
    done = pl.pallas_call(
        kernel,
        out_shape=outs,
        in_specs=[whole] * 3,
        out_specs=(whole,) * 3,
        scratch_shapes=[pltpu.VMEM(s, BF16) for s in bf16s]
        + [pltpu.VMEM(s, BF16 if s[-2] == CODE else F32) for s in sums]
        + [pltpu.SemaphoreType.DMA((N_MSG,)), pltpu.SemaphoreType.DMA((N_MSG,)), pltpu.SemaphoreType.DMA((20,))],
        compiler_params=pltpu.CompilerParams(
            collective_id=0, has_side_effects=True, vmem_limit_bytes=40 * 2**20
        ),
        name="projection",
    )(attn, w, cot)
    return pl.pallas_call(
        pass_on,
        out_shape=[jax.ShapeDtypeStruct(o.shape, o.dtype) for o in done],
        in_specs=[whole] * 3,
        out_specs=[whole] * 3,
        scratch_shapes=[pltpu.SemaphoreType.DMA((3,))],
        name="results",
    )(*(pltpu.with_memory_space_constraint(o, pltpu.VMEM) for o in done))


def solution(mesh):
    in_specs = (P(("depth", "row"), "col"), P("row", "col"), P(("depth", "row"), "col"))
    out_specs = (P(("depth", "row"), "col"), P(("depth", "row"), "col"), P("row", "col"))
    return jax.shard_map(body, mesh=mesh, in_specs=in_specs, out_specs=out_specs, check_vma=False)
```
